128 devices in a mesh: sec: 8 (over x, core), key: 16 (over y, z).
Axes of the slice: x: 4, y: 4, z: 4, core: 2. Of those that a mesh axis runs over, the one named last changes fastest.
Arguments:
- query: bfloat16 [16384, 16, 128], P(('sec', 'key')), may hold values from -64 to 64
- key: bfloat16 [16384, 4, 128], P(('sec', 'key')), may hold values from -5 to 5
- value: bfloat16 [16384, 4, 128], P(('sec', 'key')), may hold values from -5 to 5
- raw_directions: bfloat16 [16384, 4, 128], P(('sec', 'key')), may hold values from -5 to 5
- beta_raw_logits: float32 [16384, 4], P(('sec', 'key')), may hold values from -7 to 7
Outputs:
- attended: bfloat16 [16384, 16, 128], P(('sec', 'key'))
The draws below stay inside these ranges and needn't reach their ends.
All inputs are finite; a program needn't handle non-finite values.
Results may differ from the reference program's by a relative error of at most 0.0055.
Values sent between devices are 32-bit elements; how exact they have to be, the bound alone decides.
A program may use at most 64 MiB of HBM per device.

```python
import jax
import jax.numpy as jnp
from jax import lax

HEAD_WIDTH = 128
QUERY_HEADS = 16
KEY_VALUE_HEADS = 4
TOKENS_PER_PART = 128
SEQUENCE_TOKENS = 16384


def head_ordering(key):
    ordering_random_key = jax.random.fold_in(jax.random.fold_in(key, 23), 0)
    return jax.random.permutation(ordering_random_key, KEY_VALUE_HEADS)


def draw_query(key, part):
    base_key = jax.random.fold_in(jax.random.fold_in(key, 11), 0)
    base = jnp.clip(jax.random.normal(base_key, (SEQUENCE_TOKENS, QUERY_HEADS, HEAD_WIDTH), jnp.float32), -4.0, 4.0)
    return base.astype(jnp.bfloat16)


def draw_raw_directions(key, part):
    token_ordering = head_ordering(key)
    quick_heads = token_ordering >= KEY_VALUE_HEADS // 2
    basis_key, pick_key, size_key, sign_key, noise_key, drawn_key = jax.random.split(jax.random.fold_in(key, 37), 6)
    basis_vectors = jnp.clip(jax.random.normal(basis_key, (KEY_VALUE_HEADS, 4, HEAD_WIDTH), jnp.float32), -3.0, 3.0)
    picked_rows = jax.random.randint(pick_key, (SEQUENCE_TOKENS, KEY_VALUE_HEADS), 0, 4)
    head_numbers = jnp.arange(KEY_VALUE_HEADS)[None, :]
    chosen_vectors = basis_vectors[head_numbers, picked_rows]
    token_signs = jnp.where(jax.random.bernoulli(sign_key, 0.5, (SEQUENCE_TOKENS, KEY_VALUE_HEADS, 1)), 1.0, -1.0)
    token_sizes = token_signs * jax.random.uniform(size_key, (SEQUENCE_TOKENS, KEY_VALUE_HEADS, 1), jnp.float32, 0.5, 1.5)
    noise_rows = jnp.clip(jax.random.normal(noise_key, (SEQUENCE_TOKENS, KEY_VALUE_HEADS, HEAD_WIDTH), jnp.float32), -4.0, 4.0)
    confined_rows = token_sizes * chosen_vectors + 0.1 * noise_rows
    drawn_rows = jnp.clip(jax.random.normal(drawn_key, (SEQUENCE_TOKENS, KEY_VALUE_HEADS, HEAD_WIDTH), jnp.float32), -5.0, 5.0)
    return jnp.where(quick_heads[None, :, None], confined_rows, drawn_rows).astype(jnp.bfloat16)


def draw_beta_raw_logits(key, part):
    signs_random_key = jax.random.fold_in(jax.random.fold_in(key, 23), 1)
    sizes_random_key = jax.random.fold_in(jax.random.fold_in(key, 23), 2)
    quick_random_key = jax.random.fold_in(jax.random.fold_in(key, 23), 3)
    token_ordering = head_ordering(key)
    slower_path = token_ordering < KEY_VALUE_HEADS // 2
    random_signs = jnp.where(jax.random.bernoulli(signs_random_key, 0.5, (SEQUENCE_TOKENS, KEY_VALUE_HEADS)), 1.0, -1.0)
    slower_value_rows = random_signs * jax.random.uniform(sizes_random_key, (SEQUENCE_TOKENS, KEY_VALUE_HEADS), jnp.float32, 4.0, 7.0)
    quick_value_rows = jax.random.uniform(quick_random_key, (SEQUENCE_TOKENS, KEY_VALUE_HEADS), jnp.float32, -2.0, 2.0)
    return jnp.where(slower_path[None, :], slower_value_rows, quick_value_rows).astype(jnp.float32)


def block_scale(own_key, extent, cuts, least, top_value):
    loudness = 1.0
    for axis_at, parts in cuts:
        draws = jax.random.uniform(jax.random.fold_in(jax.random.fold_in(own_key, 6), axis_at), (parts,), jnp.float32, least / len(cuts), top_value / len(cuts))
        loudness = loudness * jnp.repeat(jnp.exp(draws), extent[axis_at] // parts).reshape((-1,) + (1,) * (len(extent) - 1 - axis_at))
    return loudness


def normal_values(rng, shape, scale, reach, pieces=(), held_as=jnp.bfloat16):
    factor_of = block_scale(rng, shape, pieces, -0.22, 0.18) if pieces else 1.0
    entries = jax.random.normal(rng, shape, jnp.float32) * scale * factor_of
    return jnp.minimum(jnp.maximum(entries, -reach), reach).astype(held_as)


def setup_inputs(seed: int = 0) -> dict:
    keys = jax.random.split(jax.random.key(seed), 6)
    query = draw_query(jax.random.fold_in(keys[5], 71), 0)
    key = normal_values(keys[1], (SEQUENCE_TOKENS, KEY_VALUE_HEADS, HEAD_WIDTH), 1.0, 5.0, ((0, 128),))
    value = normal_values(keys[2], (SEQUENCE_TOKENS, KEY_VALUE_HEADS, HEAD_WIDTH), 1.0, 5.0, ((0, 128),))
    raw_directions = draw_raw_directions(jax.random.fold_in(keys[5], 71), 0)
    beta_raw_logits = draw_beta_raw_logits(jax.random.fold_in(keys[5], 71), 0)
    return dict(query=query, key=key, value=value, raw_directions=raw_directions, beta_raw_logits=beta_raw_logits)


highest = lax.Precision.HIGHEST

def block_terms(query, key, raw_directions, beta_raw_logits):
    length = key.shape[0]
    heads = key.shape[1]
    width = key.shape[2]
    query_group = query.shape[1] // heads
    w_float = raw_directions.astype(jnp.float32)
    w_unit = w_float / jnp.sqrt(lax.optimization_barrier(jnp.sum(w_float * w_float, -1, keepdims=True)) + 1e-06)
    beta = 2.0 * jax.nn.sigmoid(beta_raw_logits)
    w_heads = jnp.transpose(w_unit, (1, 0, 2))
    k_heads = jnp.transpose(key.astype(jnp.float32), (1, 0, 2))
    b_heads = jnp.transpose(beta, (1, 0))[:, :, None]
    positions = jnp.arange(length)
    strict = (positions[:, None] > positions[None, :]).astype(jnp.float32)
    lower = (positions[:, None] >= positions[None, :]).astype(jnp.float32)
    gram = jnp.einsum('hte,hse->hts', w_heads, w_heads, precision=highest) * strict
    system = jnp.eye(length, dtype=jnp.float32) + b_heads * gram
    cross = jnp.einsum('hte,hse->hts', w_heads, k_heads, precision=highest) * strict
    right = jnp.concatenate([b_heads * w_heads, b_heads * cross], axis=2)
    solved = lax.linalg.triangular_solve(system, right, left_side=True, lower=True, unit_diagonal=True)
    y_rows = solved[:, :, :width]
    z_rows = solved[:, :, width:]
    block_map = jnp.eye(width, dtype=jnp.float32) - jnp.einsum('hte,htf->hef', w_heads, y_rows, precision=highest)
    key_end = k_heads - jnp.einsum('hts,hte->hse', z_rows, w_heads, precision=highest)
    q_heads = jnp.transpose(query.astype(jnp.float32).reshape(length, heads, query_group, width), (1, 2, 0, 3))
    q_dot_w = jnp.einsum('hgie,hte->hgit', q_heads, w_heads, precision=highest) * lower
    query_start = q_heads - jnp.einsum('hgit,hte->hgie', q_dot_w, y_rows, precision=highest)
    inner = jnp.einsum('hgie,hje->hgij', q_heads, k_heads, precision=highest)
    inner = inner - jnp.einsum('hgit,htj->hgij', q_dot_w, z_rows, precision=highest)
    query_start = query_start.reshape(heads, query_group * length, width)
    inner = inner.reshape(heads, query_group * length, length) * width ** (-0.5)
    return (query_start, key_end, block_map, inner)

def attend(state, scores, values, valid):
    score_maxima, weighted_totals, exponent_sums = state
    masked = jnp.where(valid, scores, -1e+30)
    new_max = jnp.maximum(score_maxima, lax.optimization_barrier(jnp.max(masked, -1)))
    weights = jnp.where(valid, jnp.exp(masked - new_max[..., None]), 0.0)
    factor = jnp.exp(score_maxima - new_max)
    weighted_totals = weighted_totals * factor + lax.optimization_barrier(jnp.sum(weights, -1))
    rounded = lax.optimization_barrier(weights.astype(jnp.bfloat16)).astype(jnp.float32)
    exponent_sums = exponent_sums * factor[..., None] + jnp.einsum('...ij,...je->...ie', rounded, values.astype(jnp.float32), precision=highest)
    return (new_max, weighted_totals, exponent_sums)

def reference(query, key, value, raw_directions, beta_raw_logits):
    block_list = SEQUENCE_TOKENS // TOKENS_PER_PART
    query_group = QUERY_HEADS // KEY_VALUE_HEADS
    q_blocks = query.reshape(block_list, TOKENS_PER_PART, QUERY_HEADS, HEAD_WIDTH)
    key_block_list = key.reshape(block_list, TOKENS_PER_PART, KEY_VALUE_HEADS, HEAD_WIDTH)
    direction_block_list = raw_directions.reshape(block_list, TOKENS_PER_PART, KEY_VALUE_HEADS, HEAD_WIDTH)
    beta_block_list = beta_raw_logits.reshape(block_list, TOKENS_PER_PART, KEY_VALUE_HEADS)
    query_start, key_end, block_map, inner = jax.vmap(block_terms)(q_blocks, key_block_list, direction_block_list, beta_block_list)
    value_head_rows = jnp.transpose(value.reshape(block_list, TOKENS_PER_PART, KEY_VALUE_HEADS, HEAD_WIDTH), (0, 2, 1, 3))
    positions = jnp.arange(TOKENS_PER_PART)
    causal = jnp.tile(positions[:, None] >= positions[None, :], (query_group, 1))
    score_maxima = jnp.full((block_list, KEY_VALUE_HEADS, query_group * TOKENS_PER_PART), -1e+30, jnp.float32)
    weighted_totals = jnp.zeros((block_list, KEY_VALUE_HEADS, query_group * TOKENS_PER_PART), jnp.float32)
    exponent_sums = jnp.zeros((block_list, KEY_VALUE_HEADS, query_group * TOKENS_PER_PART, HEAD_WIDTH), jnp.float32)
    score_maxima, weighted_totals, exponent_sums = attend((score_maxima, weighted_totals, exponent_sums), inner, value_head_rows, causal)
    block_ids = jnp.arange(block_list)

    def advance(step, carry):
        score_maxima, weighted_totals, exponent_sums, moving = carry
        keys_back = jnp.roll(key_end, step, axis=0)
        values_back = jnp.roll(value_head_rows, step, axis=0)
        maps_back = jnp.roll(block_map, step, axis=0)
        scores = jnp.einsum('nhie,nhje->nhij', moving, keys_back, precision=highest) * HEAD_WIDTH ** (-0.5)
        valid = (block_ids >= step)[:, None, None, None]
        score_maxima, weighted_totals, exponent_sums = attend((score_maxima, weighted_totals, exponent_sums), scores, values_back, valid)
        moving = jnp.einsum('nhie,nhef->nhif', moving, maps_back, precision=highest)
        return (score_maxima, weighted_totals, exponent_sums, moving)
    score_maxima, weighted_totals, exponent_sums, moving = lax.fori_loop(1, block_list, advance, (score_maxima, weighted_totals, exponent_sums, query_start))
    final_output = exponent_sums / weighted_totals[..., None]
    final_output = final_output.reshape(block_list, KEY_VALUE_HEADS, query_group, TOKENS_PER_PART, HEAD_WIDTH)
    final_output = jnp.transpose(final_output, (0, 3, 1, 2, 4)).reshape(SEQUENCE_TOKENS, QUERY_HEADS, HEAD_WIDTH)
    return final_output.astype(jnp.bfloat16)
```

```python
import functools
import math

import jax
import jax.numpy as jnp
from jax import lax
from jax.experimental import pallas as pl
from jax.experimental.pallas import tpu as pltpu
from jax.sharding import PartitionSpec as P

F32 = jnp.float32
BF16 = jnp.bfloat16
NN = ((1,), (0,))
NT = ((1,), (1,))
TN = ((0,), (0,))
LOW = -1e30
VMEM_LIMIT = 56 * 1024 * 1024
WIDE = 8


def halves(x):
    high = x.astype(BF16)
    return high, (x - high.astype(F32)).astype(BF16)


def left(x, axis):
    high, low = halves(x)
    return jnp.concatenate([high, low, high, low], axis)


def right(x, axis):
    high, low = halves(x)
    return jnp.concatenate([high, high, low, low], axis)


def mm(a, b, dims):
    return lax.dot_general(a, b, (dims, ((), ())), preferred_element_type=F32)


def fine(a, b, dims):
    return mm(left(a, dims[0][0]), right(b, dims[1][0]), dims)


def grids(n):
    return lax.broadcasted_iota(jnp.int32, (n, n), 0), lax.broadcasted_iota(jnp.int32, (n, n), 1)


def as_row(column, eye):
    return jnp.sum(jnp.where(eye, column, 0.0), 0, keepdims=True)


def as_column(row, eye):
    return jnp.sum(jnp.where(eye, row, 0.0), 1, keepdims=True)


def terms_kernel(scale, q_ref, k_ref, v_ref, w_ref, b_ref, x_ref, z_ref, qw_ref):
    heads, n, width = k_ref.shape
    group = q_ref.shape[0] // heads
    row, col = grids(n)
    units, betas, lows, inverses = [], [], [], []
    for h in range(heads):
        w = w_ref[h].astype(F32)
        unit = w / jnp.sqrt(jnp.sum(w * w, -1, keepdims=True) + 1e-6)
        beta = 2.0 / (1.0 + jnp.exp(-b_ref[:, h : h + 1]))
        low = jnp.where(row > col, beta * fine(unit, unit, NT), 0.0)
        first = ((row ^ col) == 1) & (row > col)
        units.append(unit)
        betas.append(beta)
        lows.append(low)
        inverses.append(jnp.where(row == col, 1.0, jnp.where(first, -low, 0.0)))
    size = 2
    while size < n:
        pick = ((row ^ col) < 2 * size) & ((row & size) != 0) & ((col & size) == 0)
        inner = [fine(jnp.where(pick, lows[h], 0.0), inverses[h], NN) for h in range(heads)]
        inverses = [inverses[h] - fine(inverses[h], inner[h], NN) for h in range(heads)]
        size *= 2
    for h in range(heads):
        unit, beta, inverse = units[h], betas[h], inverses[h]
        key = k_ref[h]
        high, low = halves(unit)
        both = jnp.concatenate([high, low], 1)
        cross = jnp.where(row > col, mm(both, jnp.concatenate([key, key], 1), NT), 0.0)
        solved = fine(inverse, jnp.concatenate([beta * unit, beta * cross], 1), NN)
        y, z = solved[:, :width], solved[:, width:]
        z_ref[h] = z
        block_map = jnp.where(row == col, 1.0, 0.0) - fine(unit, y, TN)
        key_end = key.astype(F32) - fine(z, unit, TN)
        value = v_ref[h].astype(F32)
        y_right = right(y, 0)
        for g in range(h * group, h * group + group):
            query = q_ref[g]
            qw = jnp.where(row >= col, mm(jnp.concatenate([query, query], 1), both, NT), 0.0)
            qw_ref[g] = qw
            x_ref[g, 0] = (query.astype(F32) - mm(left(qw, 1), y_right, NN)) * scale
            x_ref[g, 1] = key_end
            x_ref[g, 2] = value
            x_ref[g, 3] = block_map


def diagonal_kernel(scale, q_ref, k_ref, v_ref, z_ref, qw_ref, o_ref, m_ref, l_ref):
    heads, n, width = k_ref.shape
    group = q_ref.shape[0] // heads
    row, col = grids(n)
    for h in range(heads):
        z_right = right(z_ref[h], 0)
        for g in range(h * group, h * group + group):
            score = mm(q_ref[g], k_ref[h], NT) - mm(left(qw_ref[g], 1), z_right, NN)
            score = jnp.where(row >= col, score * scale, LOW)
            top = jnp.max(score, -1, keepdims=True)
            weight = jnp.exp2(score - top)
            m_ref[g] = top
            l_ref[g] = jnp.sum(weight, -1, keepdims=True)
            o_ref[g] = mm(weight.astype(BF16), v_ref[h], NN)


def frames_kernel(x_ref, q_ref, kv_ref, s_ref):
    blocks, _, n, width = x_ref.shape
    before, after = None, None
    for a in range(blocks):
        b = blocks - 1 - a
        query, key = x_ref[a, 0], x_ref[b, 1]
        kv_ref[b * n : b * n + n, width:] = x_ref[b, 2]
        if a == 0:
            q_ref[:n] = query
            kv_ref[b * n : b * n + n, :width] = key
            before, after = x_ref[a, 3], x_ref[b, 3]
        else:
            q_ref[a * n : a * n + n] = fine(query, before, NN)
            kv_ref[b * n : b * n + n, :width] = fine(key, after, NT)
            before, after = fine(x_ref[a, 3], before, NN), fine(after, x_ref[b, 3], NN)
    s_ref[...] = before


def near_kernel(x_ref, o_ref, m_ref, l_ref, key_ref, cat_ref, value_ref):
    blocks, _, n, width = x_ref.shape
    o_ref[:n] = jnp.zeros((n, width), F32)
    m_ref[:n] = jnp.full((n, 1), LOW, F32)
    l_ref[:n] = jnp.zeros((n, 1), F32)
    for a in range(1, blocks):
        last, rows = (a - 1) * n, a * n
        if a > 1:
            key_ref[:last] = mm(cat_ref[:last], left(x_ref[a - 1, 3], 1), NT)
        key_ref[last:rows] = x_ref[a - 1, 1]
        value_ref[last:rows] = x_ref[a - 1, 2].astype(BF16)
        cat_ref[:rows] = right(key_ref[:rows], 1)
        score = mm(left(x_ref[a, 0], 1), cat_ref[:rows], NT)
        top = jnp.max(score, -1, keepdims=True)
        weight = jnp.exp2(score - top)
        m_ref[rows : rows + n] = top
        l_ref[rows : rows + n] = jnp.sum(weight, -1, keepdims=True)
        o_ref[rows : rows + n] = mm(weight.astype(BF16), value_ref[:rows], NN)


def far_kernel(q_in, kv_hbm, maps_ref, o_in, m_in, l_in, out_ref, q_ref, o_ref, m_ref, l_ref, kv_ref, cat_ref, value_ref, sems):
    blocks, _, width = out_ref.shape
    n = width
    rows = q_in.shape[0]
    step = 256
    mine = lax.axis_index("sec")
    q_ref[...] = left(q_in[...], 1)
    o_ref[...] = o_in[...]
    m_ref[...] = m_in[...]
    l_ref[...] = l_in[...]

    def fetch(index):
        return pltpu.make_async_copy(kv_hbm.at[mine - 1 - index], kv_ref.at[index % 2], sems.at[index % 2])

    @pl.when(mine > 0)
    def _():
        fetch(0).start()

    def walk(index, carry):
        fetch(index).wait()

        @pl.when(index + 1 < mine)
        def _():
            fetch(index + 1).start()

        slot = index % 2
        cat_ref[...] = right(kv_ref[slot, :, :width], 1)
        value_ref[...] = kv_ref[slot, :, width:].astype(BF16)
        turn = right(maps_ref[mine - 1 - index], 0)

        def part(at, carry):
            here = pl.ds(pl.multiple_of(at * step, step), step)
            query = q_ref[here, :]
            score = mm(query, cat_ref[...], NT)
            old = m_ref[here, :]
            top = jnp.maximum(old, jnp.max(score, -1, keepdims=True))
            weight = jnp.exp2(score - top)
            factor = jnp.exp2(old - top)
            m_ref[here, :] = top
            l_ref[here, :] = l_ref[here, :] * factor + jnp.sum(weight, -1, keepdims=True)
            o_ref[here, :] = o_ref[here, :] * factor + mm(weight.astype(BF16), value_ref[...], NN)
            q_ref[here, :] = left(mm(query, turn, NN), 1)
            return carry

        return lax.fori_loop(0, rows // step, part, carry)

    lax.fori_loop(0, mine, walk, 0)
    row, col = grids(n)
    for a in range(blocks):
        here = slice(a * n, a * n + n)
        out_ref[a, :n] = o_ref[here]
        out_ref[a, n : n + 1] = as_row(m_ref[here], row == col)
        out_ref[a, n + 1 : n + 2] = as_row(l_ref[here], row == col)
        out_ref[a, n + 2 :] = jnp.zeros((WIDE - 2, width), F32)


def merge_kernel(far_ref, o_ref, m_ref, l_ref, out_ref):
    heads, n, width = o_ref.shape
    row, col = grids(n)
    for g in range(heads):
        far_top = as_column(far_ref[g, n : n + 1], row == col)
        far_sum = as_column(far_ref[g, n + 1 : n + 2], row == col)
        near_top = m_ref[g]
        top = jnp.maximum(far_top, near_top)
        far_factor, near_factor = jnp.exp2(far_top - top), jnp.exp2(near_top - top)
        total = far_sum * far_factor + l_ref[g] * near_factor
        mixed = far_ref[g, :n] * far_factor + o_ref[g] * near_factor
        out_ref[g] = (mixed / total).astype(BF16)


def shape(*dims, dtype=F32):
    return jax.ShapeDtypeStruct(dims, dtype)


def call(kernel, out_shape, *operands, scratch=(), in_specs=None, **params):
    return pl.pallas_call(
        kernel,
        out_shape=out_shape,
        in_specs=in_specs or [pl.BlockSpec(memory_space=pltpu.VMEM)] * len(operands),
        out_specs=jax.tree.map(lambda _: pl.BlockSpec(memory_space=pltpu.VMEM), out_shape),
        scratch_shapes=list(scratch),
        compiler_params=pltpu.CompilerParams(vmem_limit_bytes=VMEM_LIMIT, **params),
    )(*operands)


def body(query, key, value, raw_directions, beta_raw_logits):
    n, heads, width = query.shape
    kv_heads = key.shape[1]
    blocks = lax.axis_size("key")
    sections = lax.axis_size("sec")
    rows = n * blocks
    scale = width ** (-0.5) * math.log2(math.e)
    q, k, v, w = (jnp.transpose(x, (1, 0, 2)) for x in (query, key, value, raw_directions))
    sent, z, qw = call(
        functools.partial(terms_kernel, scale),
        [shape(heads, 4, n, width), shape(kv_heads, n, n), shape(heads, n, n)],
        q, k, v, w, beta_raw_logits,
    )
    near = lax.all_to_all(sent, "key", split_axis=0, concat_axis=0, tiled=True)
    own = call(
        functools.partial(diagonal_kernel, scale),
        [shape(heads, n, width), shape(heads, n, 1), shape(heads, n, 1)],
        q, k, v, z, qw,
    )
    section_query, section_kv, section_map = call(
        frames_kernel, [shape(rows, width), shape(rows, 2 * width), shape(width, width)], near
    )
    all_kv = lax.all_gather(section_kv, "sec")
    all_maps = lax.all_gather(section_map, "sec")
    state = call(
        near_kernel,
        [shape(rows, width), shape(rows, 1), shape(rows, 1)],
        near,
        scratch=[pltpu.VMEM((rows, width), F32), pltpu.VMEM((rows, 4 * width), BF16), pltpu.VMEM((rows, width), BF16)],
    )
    vmem = pl.BlockSpec(memory_space=pltpu.VMEM)
    back = call(
        far_kernel,
        shape(blocks, n + WIDE, width),
        section_query, all_kv, all_maps, *state,
        in_specs=[vmem, pl.BlockSpec(memory_space=pl.ANY)] + [vmem] * 4,
        scratch=[
            pltpu.VMEM((rows, 4 * width), BF16),
            pltpu.VMEM((rows, width), F32),
            pltpu.VMEM((rows, 1), F32),
            pltpu.VMEM((rows, 1), F32),
            pltpu.VMEM((2, rows, 2 * width), F32),
            pltpu.VMEM((rows, 4 * width), BF16),
            pltpu.VMEM((rows, width), BF16),
            pltpu.SemaphoreType.DMA((2,)),
        ],
    )
    far = lax.all_to_all(back, "key", split_axis=0, concat_axis=0, tiled=True)
    merged = call(merge_kernel, shape(heads, n, width, dtype=BF16), far, *own)
    return jnp.transpose(merged, (1, 0, 2))


def solution(mesh):
    spec = P(("sec", "key"), None, None)
    return jax.shard_map(
        body,
        mesh=mesh,
        in_specs=(spec, spec, spec, spec, P(("sec", "key"), None)),
        out_specs=spec,
        check_vma=False,
    )
```

```python
import functools
import math

import jax
import jax.numpy as jnp
from jax import lax
from jax.experimental import pallas as pl
from jax.experimental.pallas import tpu as pltpu
from jax.sharding import PartitionSpec as P

F32 = jnp.float32
BF16 = jnp.bfloat16
NN = ((1,), (0,))
NT = ((1,), (1,))
TN = ((0,), (0,))
LOW = -1e30
VMEM_LIMIT = 56 * 1024 * 1024
WIDE = 8


def halves(x):
    high = x.astype(BF16)
    return high, (x - high.astype(F32)).astype(BF16)


def left(x, axis):
    high, low = halves(x)
    return jnp.concatenate([high, low, high, low], axis)


def right(x, axis):
    high, low = halves(x)
    return jnp.concatenate([high, high, low, low], axis)


def mm(a, b, dims):
    return lax.dot_general(a, b, (dims, ((), ())), preferred_element_type=F32)


def fine(a, b, dims):
    return mm(left(a, dims[0][0]), right(b, dims[1][0]), dims)


def grids(n):
    return lax.broadcasted_iota(jnp.int32, (n, n), 0), lax.broadcasted_iota(jnp.int32, (n, n), 1)


def as_row(column, eye):
    return jnp.sum(jnp.where(eye, column, 0.0), 0, keepdims=True)


def as_column(row, eye):
    return jnp.sum(jnp.where(eye, row, 0.0), 1, keepdims=True)


def terms_kernel(scale, q_ref, k_ref, v_ref, w_ref, b_ref, x_ref, z_ref, qw_ref):
    heads, n, width = k_ref.shape
    group = q_ref.shape[0] // heads
    row, col = grids(n)
    units, betas, lows, inverses = [], [], [], []
    for h in range(heads):
        w = w_ref[h].astype(F32)
        unit = w / jnp.sqrt(jnp.sum(w * w, -1, keepdims=True) + 1e-6)
        beta = 2.0 / (1.0 + jnp.exp(-b_ref[:, h : h + 1]))
        low = jnp.where(row > col, beta * fine(unit, unit, NT), 0.0)
        first = ((row ^ col) == 1) & (row > col)
        units.append(unit)
        betas.append(beta)
        lows.append(low)
        inverses.append(jnp.where(row == col, 1.0, jnp.where(first, -low, 0.0)))
    size = 2
    while size < n:
        pick = ((row ^ col) < 2 * size) & ((row & size) != 0) & ((col & size) == 0)
        inner = [fine(jnp.where(pick, lows[h], 0.0), inverses[h], NN) for h in range(heads)]
        inverses = [inverses[h] - fine(inverses[h], inner[h], NN) for h in range(heads)]
        size *= 2
    for h in range(heads):
        unit, beta, inverse = units[h], betas[h], inverses[h]
        key = k_ref[h]
        high, low = halves(unit)
        both = jnp.concatenate([high, low], 1)
        cross = jnp.where(row > col, mm(both, jnp.concatenate([key, key], 1), NT), 0.0)
        solved = fine(inverse, jnp.concatenate([beta * unit, beta * cross], 1), NN)
        y, z = solved[:, :width], solved[:, width:]
        z_ref[h] = z
        block_map = jnp.where(row == col, 1.0, 0.0) - fine(unit, y, TN)
        key_end = key.astype(F32) - fine(z, unit, TN)
        value = v_ref[h].astype(F32)
        y_right = right(y, 0)
        for g in range(h * group, h * group + group):
            query = q_ref[g]
            qw = jnp.where(row >= col, mm(jnp.concatenate([query, query], 1), both, NT), 0.0)
            qw_ref[g] = qw
            x_ref[g, 0] = (query.astype(F32) - mm(left(qw, 1), y_right, NN)) * scale
            x_ref[g, 1] = key_end
            x_ref[g, 2] = value
            x_ref[g, 3] = block_map


def diagonal_kernel(scale, q_ref, k_ref, v_ref, z_ref, qw_ref, o_ref, m_ref, l_ref):
    heads, n, width = k_ref.shape
    group = q_ref.shape[0] // heads
    row, col = grids(n)
    for h in range(heads):
        z_right = right(z_ref[h], 0)
        for g in range(h * group, h * group + group):
            score = mm(q_ref[g], k_ref[h], NT) - mm(left(qw_ref[g], 1), z_right, NN)
            score = jnp.where(row >= col, score * scale, LOW)
            top = jnp.max(score, -1, keepdims=True)
            weight = jnp.exp2(score - top)
            m_ref[g] = top
            l_ref[g] = jnp.sum(weight, -1, keepdims=True)
            o_ref[g] = mm(weight.astype(BF16), v_ref[h], NN)


def frames_kernel(x_ref, q_ref, kv_ref, s_ref):
    blocks, _, n, width = x_ref.shape
    before, after = None, None
    for a in range(blocks):
        b = blocks - 1 - a
        query, key = x_ref[a, 0], x_ref[b, 1]
        kv_ref[b * n : b * n + n, width:] = x_ref[b, 2]
        if a == 0:
            q_ref[:n] = query
            kv_ref[b * n : b * n + n, :width] = key
            before, after = x_ref[a, 3], x_ref[b, 3]
        else:
            q_ref[a * n : a * n + n] = fine(query, before, NN)
            kv_ref[b * n : b * n + n, :width] = fine(key, after, NT)
            before, after = fine(x_ref[a, 3], before, NN), fine(after, x_ref[b, 3], NN)
    s_ref[...] = before


def near_attention(x_ref, key_ref, cat_ref, value_ref, store, between):
    blocks, _, n, width = x_ref.shape
    store(0, jnp.zeros((n, width), F32), jnp.full((n, 1), LOW, F32), jnp.zeros((n, 1), F32))
    for a in range(1, blocks):
        last, rows = (a - 1) * n, a * n
        if a > 1:
            key_ref[:last] = mm(cat_ref[:last], left(x_ref[a - 1, 3], 1), NT)
        key_ref[last:rows] = x_ref[a - 1, 1]
        value_ref[last:rows] = x_ref[a - 1, 2].astype(BF16)
        cat_ref[:rows] = right(key_ref[:rows], 1)
        score = mm(left(x_ref[a, 0], 1), cat_ref[:rows], NT)
        top = jnp.max(score, -1, keepdims=True)
        weight = jnp.exp2(score - top)
        store(a, mm(weight.astype(BF16), value_ref[:rows], NN), top, jnp.sum(weight, -1, keepdims=True))
        between(a)


def section_kernel(
    x_ref, q_in, kv_ref, map_ref, out_ref,
    all_kv, maps, frames, partner_q, turning, key_ref, cat_ref, value_ref,
    o_ref, m_ref, l_ref, high_o, high_m, high_l, pack, partner_pack,
    local_sem, kv_send, kv_recv, map_send, map_recv, q_sems, pack_sems,
):
    blocks, _, n, width = x_ref.shape
    rows, half = blocks * n, blocks * n // 2
    quarter_rows, step = rows // 4, 256
    sections = all_kv.shape[0]
    chips = sections // 2
    s, k = lax.axis_index("sec"), lax.axis_index("key")
    x, c = s // 2, s % 2
    z = k % 4
    sibling, partner = s + 1 - 2 * c, sections - 1 - s
    ahead, behind, across = ((x + d) % chips * 2 + c for d in (1, chips - 1, chips // 2))
    z_next, z_last = k - z + (z + 1) % 4, k - z + (z + 3) % 4
    mine, other = z % 2 * 2, 2 - z % 2 * 2

    def place(t, quarter):
        return all_kv.at[t, pl.ds(pl.multiple_of(quarter * quarter_rows, quarter_rows), quarter_rows)]

    sent = []

    def put(t, quarter, device, source=None):
        copy = pltpu.make_async_remote_copy(
            src_ref=place(t, quarter) if source is None else source,
            dst_ref=place(t, quarter),
            send_sem=kv_send.at[len(sent)],
            recv_sem=kv_recv.at[t, quarter],
            device_id=device,
            device_id_type=pl.DeviceIdType.MESH,
        )
        copy.start()
        sent.append(copy)

    def got(t, quarter):
        pltpu.make_async_remote_copy(
            src_ref=place(t, quarter),
            dst_ref=place(t, quarter),
            send_sem=kv_send.at[0],
            recv_sem=kv_recv.at[t, quarter],
            device_id=(sibling, k),
            device_id_type=pl.DeviceIdType.MESH,
        ).wait_recv()

    others = [(s + d) % sections for d in range(1, sections)]
    barrier = pltpu.get_barrier_semaphore()
    greeted = [(t, k) for t in others] + [(s, z_next), (s, z_last)]
    for device in greeted:
        pl.semaphore_signal(barrier, inc=1, device_id=device, device_id_type=pl.DeviceIdType.MESH)
    pl.semaphore_wait(barrier, len(greeted))

    map_copies = [
        pltpu.make_async_remote_copy(
            src_ref=map_ref,
            dst_ref=maps.at[s],
            send_sem=map_send.at[d],
            recv_sem=map_recv.at[s],
            device_id=(t, k),
            device_id_type=pl.DeviceIdType.MESH,
        )
        for d, t in enumerate(others)
    ]
    for copy in map_copies:
        copy.start()
    query_copy = pltpu.make_async_remote_copy(
        src_ref=q_in.at[half:],
        dst_ref=partner_q,
        send_sem=q_sems.at[0],
        recv_sem=q_sems.at[1],
        device_id=(partner, k),
        device_id_type=pl.DeviceIdType.MESH,
    )
    query_copy.start()
    own_copy = pltpu.make_async_copy(kv_ref, all_kv.at[s], local_sem)
    own_copy.start()
    for index in range(2):
        source = kv_ref.at[pl.ds(pl.multiple_of((mine + index) * quarter_rows, quarter_rows), quarter_rows)]
        put(s, mine + index, (ahead, k), source)
        put(s, mine + index, (behind, k), source)
    for quarter in range(4):
        put(s, quarter, (sibling, k), kv_ref.at[quarter * quarter_rows : (quarter + 1) * quarter_rows])

    def pass_mine(t, index, onward):
        got(t, mine + index)
        if onward is not None:
            put(t, mine + index, (onward, k))
        put(t, mine + index, (s, z_last if index else z_next))
        put(t, mine + index, (sibling, k))

    def pass_other(t, index):
        got(t, other + index)
        put(t, other + index, (sibling, k))

    def between(a):
        if a == 9:
            pass_mine(behind, 0, ahead)
            pass_mine(ahead, 0, None)
        if a == 13:
            pass_mine(behind, 1, None)
            pass_mine(ahead, 1, behind)

    def store(a, o, m, l):
        at = slice(a % (blocks // 2) * n, a % (blocks // 2) * n + n)
        if a < blocks // 2:
            o_ref[at], m_ref[at], l_ref[at] = o, m, l
        else:
            high_o[at], high_m[at], high_l[at] = o, m, l

    near_attention(x_ref, key_ref, cat_ref, value_ref, store, between)
    o_ref[half:] = jnp.zeros((half, width), F32)
    m_ref[half:] = jnp.full((half, 1), LOW, F32)
    l_ref[half:] = jnp.zeros((half, 1), F32)

    maps[s] = map_ref[...]
    for d, t in enumerate(others):
        map_copies[d].wait_send()
        pltpu.make_async_remote_copy(
            src_ref=map_ref,
            dst_ref=maps.at[t],
            send_sem=map_send.at[d],
            recv_sem=map_recv.at[t],
            device_id=(t, k),
            device_id_type=pl.DeviceIdType.MESH,
        ).wait_recv()

    def build(count, base):
        def turn(index, carry):
            t = count - 1 - index
            frames[base + t] = left(turning[...], 1)

            @pl.when(t > 0)
            def _():
                turning[...] = mm(frames[base + t], right(maps[t], 0), NN)

            return carry

        lax.fori_loop(0, count, turn, 0)

    turning[...] = q_in[:half]
    build(s, 0)
    query_copy.wait()
    turning[...] = partner_q[...]
    build(partner, s)
    own_copy.wait()

    def attend(frame, first):
        def part(at, carry):
            here = pl.ds(pl.multiple_of(first + at * step, step), step)
            score = mm(frames[frame, pl.ds(pl.multiple_of(at * step, step), step), :], cat_ref[...], NT)
            old = m_ref[here, :]
            top = jnp.maximum(old, jnp.max(score, -1, keepdims=True))
            weight = jnp.exp2(score - top)
            factor = jnp.exp2(old - top)
            m_ref[here, :] = top
            l_ref[here, :] = l_ref[here, :] * factor + jnp.sum(weight, -1, keepdims=True)
            o_ref[here, :] = o_ref[here, :] * factor + mm(weight.astype(BF16), value_ref[...], NN)
            return carry

        lax.fori_loop(0, half // step, part, 0)

    def tile(t):
        @pl.when((t < s) | (t < partner))
        def _():
            cat_ref[...] = right(all_kv[t, :, :width], 1)
            value_ref[...] = all_kv[t, :, width:].astype(BF16)

        def one(which, carry):
            count = which * partner + (1 - which) * s

            @pl.when(t < count)
            def _():
                attend(which * s + t, which * half)

            return carry

        lax.fori_loop(0, 2, one, 0)

    tile(s)
    for quarter in range(4):
        got(sibling, quarter)
    tile(sibling)
    for index in range(2):
        pass_other(ahead, index)
        pass_other(behind, index)

    def beside(t):
        return t + 1 - 2 * c

    tile(ahead)
    for index in range(2):
        pass_mine(across, index, None)
    for quarter in range(4):
        got(beside(ahead), quarter)
    tile(beside(ahead))
    tile(behind)
    for index in range(2):
        pass_other(across, index)
    for quarter in range(4):
        got(beside(behind), quarter)
    tile(beside(behind))
    tile(across)
    for quarter in range(4):
        got(beside(across), quarter)
    tile(beside(across))

    row, col = grids(n)
    eye = row == col

    def packed(target, a, o, m, l):
        target[a, :n] = o
        target[a, n : n + 1] = as_row(m, eye)
        target[a, n + 1 : n + 2] = as_row(l, eye)
        target[a, n + 2 :] = jnp.zeros((WIDE - 2, width), F32)

    for a in range(blocks // 2):
        here = slice(half + a * n, half + a * n + n)
        packed(pack, a, o_ref[here], m_ref[here], l_ref[here])
    pack_copy = pltpu.make_async_remote_copy(
        src_ref=pack,
        dst_ref=partner_pack,
        send_sem=pack_sems.at[0],
        recv_sem=pack_sems.at[1],
        device_id=(partner, k),
        device_id_type=pl.DeviceIdType.MESH,
    )
    pack_copy.start()
    for a in range(blocks // 2):
        here = slice(a * n, a * n + n)
        packed(out_ref, a, o_ref[here], m_ref[here], l_ref[here])
    for copy in sent:
        copy.wait_send()
    pack_copy.wait()
    for a in range(blocks // 2):
        here = slice(a * n, a * n + n)
        far_top = as_column(partner_pack[a, n : n + 1], eye)
        far_sum = as_column(partner_pack[a, n + 1 : n + 2], eye)
        top = jnp.maximum(far_top, high_m[here])
        far_factor, factor = jnp.exp2(far_top - top), jnp.exp2(high_m[here] - top)
        o = partner_pack[a, :n] * far_factor + high_o[here] * factor
        packed(out_ref, blocks // 2 + a, o, top, far_sum * far_factor + high_l[here] * factor)


def merge_kernel(far_ref, o_ref, m_ref, l_ref, out_ref):
    heads, n, width = o_ref.shape
    row, col = grids(n)
    for g in range(heads):
        far_top = as_column(far_ref[g, n : n + 1], row == col)
        far_sum = as_column(far_ref[g, n + 1 : n + 2], row == col)
        near_top = m_ref[g]
        top = jnp.maximum(far_top, near_top)
        far_factor, near_factor = jnp.exp2(far_top - top), jnp.exp2(near_top - top)
        total = far_sum * far_factor + l_ref[g] * near_factor
        mixed = far_ref[g, :n] * far_factor + o_ref[g] * near_factor
        out_ref[g] = (mixed / total).astype(BF16)


def shape(*dims, dtype=F32):
    return jax.ShapeDtypeStruct(dims, dtype)


def call(kernel, out_shape, *operands, scratch=(), in_specs=None, **params):
    return pl.pallas_call(
        kernel,
        out_shape=out_shape,
        in_specs=in_specs or [pl.BlockSpec(memory_space=pltpu.VMEM)] * len(operands),
        out_specs=jax.tree.map(lambda _: pl.BlockSpec(memory_space=pltpu.VMEM), out_shape),
        scratch_shapes=list(scratch),
        compiler_params=pltpu.CompilerParams(vmem_limit_bytes=VMEM_LIMIT, **params),
    )(*operands)


def body(query, key, value, raw_directions, beta_raw_logits):
    n, heads, width = query.shape
    kv_heads = key.shape[1]
    blocks = lax.axis_size("key")
    sections = lax.axis_size("sec")
    rows = n * blocks
    scale = width ** (-0.5) * math.log2(math.e)
    q, k, v, w = (jnp.transpose(x, (1, 0, 2)) for x in (query, key, value, raw_directions))
    sent, z, qw = call(
        functools.partial(terms_kernel, scale),
        [shape(heads, 4, n, width), shape(kv_heads, n, n), shape(heads, n, n)],
        q, k, v, w, beta_raw_logits,
    )
    near = lax.all_to_all(sent, "key", split_axis=0, concat_axis=0, tiled=True)
    own = call(
        functools.partial(diagonal_kernel, scale),
        [shape(heads, n, width), shape(heads, n, 1), shape(heads, n, 1)],
        q, k, v, z, qw,
    )
    section_query, section_kv, section_map = call(
        frames_kernel, [shape(rows, width), shape(rows, 2 * width), shape(width, width)], near
    )
    half = rows // 2
    vmem, dma = pltpu.VMEM, pltpu.SemaphoreType.DMA
    back = call(
        section_kernel,
        shape(blocks, n + WIDE, width),
        near, section_query, section_kv, section_map,
        scratch=[
            vmem((sections, rows, 2 * width), F32),
            vmem((sections, width, width), F32),
            vmem((sections - 1, half, 4 * width), BF16),
            vmem((half, width), F32),
            vmem((half, width), F32),
            vmem((rows, width), F32),
            vmem((rows, 4 * width), BF16),
            vmem((rows, width), BF16),
            vmem((rows, width), F32),
            vmem((rows, 1), F32),
            vmem((rows, 1), F32),
            vmem((half, width), F32),
            vmem((half, 1), F32),
            vmem((half, 1), F32),
            vmem((blocks // 2, n + WIDE, width), F32),
            vmem((blocks // 2, n + WIDE, width), F32),
            dma,
            dma((28,)),
            dma((sections, 4)),
            dma((sections - 1,)),
            dma((sections,)),
            dma((2,)),
            dma((2,)),
        ],
        collective_id=0,
        has_side_effects=True,
    )
    far = lax.all_to_all(back, "key", split_axis=0, concat_axis=0, tiled=True)
    merged = call(merge_kernel, shape(heads, n, width, dtype=BF16), far, *own)
    return jnp.transpose(merged, (1, 0, 2))


def solution(mesh):
    spec = P(("sec", "key"), None, None)
    return jax.shard_map(
        body,
        mesh=mesh,
        in_specs=(spec, spec, spec, spec, P(("sec", "key"), None)),
        out_specs=spec,
        check_vma=False,
    )
```

```python
import functools
import math

import jax
import jax.numpy as jnp
from jax import lax
from jax.experimental import pallas as pl
from jax.experimental.pallas import tpu as pltpu
from jax.sharding import PartitionSpec as P

F32 = jnp.float32
BF16 = jnp.bfloat16
NN = ((1,), (0,))
NT = ((1,), (1,))
TN = ((0,), (0,))
LOW = -1e30
VMEM_LIMIT = 56 * 1024 * 1024
WIDE = 8


def halves(x):
    high = x.astype(BF16)
    return high, (x - high.astype(F32)).astype(BF16)


def left(x, axis):
    high, low = halves(x)
    return jnp.concatenate([high, low, high, low], axis)


def right(x, axis):
    high, low = halves(x)
    return jnp.concatenate([high, high, low, low], axis)


def mm(a, b, dims):
    return lax.dot_general(a, b, (dims, ((), ())), preferred_element_type=F32)


def fine(a, b, dims):
    return mm(left(a, dims[0][0]), right(b, dims[1][0]), dims)


def grids(n):
    return lax.broadcasted_iota(jnp.int32, (n, n), 0), lax.broadcasted_iota(jnp.int32, (n, n), 1)


def as_row(column, eye):
    return jnp.sum(jnp.where(eye, column, 0.0), 0, keepdims=True)


def as_column(row, eye):
    return jnp.sum(jnp.where(eye, row, 0.0), 1, keepdims=True)


def terms_kernel(scale, q_ref, k_ref, v_ref, w_ref, b_ref, x_ref, z_ref, qw_ref):
    heads, n, width = k_ref.shape
    group = q_ref.shape[0] // heads
    row, col = grids(n)
    units, betas, lows, inverses = [], [], [], []
    for h in range(heads):
        w = w_ref[h].astype(F32)
        unit = w / jnp.sqrt(jnp.sum(w * w, -1, keepdims=True) + 1e-6)
        beta = 2.0 / (1.0 + jnp.exp(-b_ref[:, h : h + 1]))
        low = jnp.where(row > col, beta * fine(unit, unit, NT), 0.0)
        first = ((row ^ col) == 1) & (row > col)
        units.append(unit)
        betas.append(beta)
        lows.append(low)
        inverses.append(jnp.where(row == col, 1.0, jnp.where(first, -low, 0.0)))
    size = 2
    while size < n:
        pick = ((row ^ col) < 2 * size) & ((row & size) != 0) & ((col & size) == 0)
        inner = [fine(jnp.where(pick, lows[h], 0.0), inverses[h], NN) for h in range(heads)]
        inverses = [inverses[h] - fine(inverses[h], inner[h], NN) for h in range(heads)]
        size *= 2
    for h in range(heads):
        unit, beta, inverse = units[h], betas[h], inverses[h]
        key = k_ref[h]
        high, low = halves(unit)
        both = jnp.concatenate([high, low], 1)
        cross = jnp.where(row > col, mm(both, jnp.concatenate([key, key], 1), NT), 0.0)
        solved = fine(inverse, jnp.concatenate([beta * unit, beta * cross], 1), NN)
        y, z = solved[:, :width], solved[:, width:]
        z_ref[h] = z
        block_map = jnp.where(row == col, 1.0, 0.0) - fine(unit, y, TN)
        key_end = key.astype(F32) - fine(z, unit, TN)
        value = v_ref[h].astype(F32)
        y_right = right(y, 0)
        for g in range(h * group, h * group + group):
            query = q_ref[g]
            qw = jnp.where(row >= col, mm(jnp.concatenate([query, query], 1), both, NT), 0.0)
            qw_ref[g] = qw
            x_ref[g, 0] = (query.astype(F32) - mm(left(qw, 1), y_right, NN)) * scale
            x_ref[g, 1] = key_end
            x_ref[g, 2] = value
            x_ref[g, 3] = block_map


def diagonal_kernel(scale, q_ref, k_ref, v_ref, z_ref, qw_ref, o_ref, m_ref, l_ref):
    heads, n, width = k_ref.shape
    group = q_ref.shape[0] // heads
    row, col = grids(n)
    for h in range(heads):
        z_right = right(z_ref[h], 0)
        for g in range(h * group, h * group + group):
            score = mm(q_ref[g], k_ref[h], NT) - mm(left(qw_ref[g], 1), z_right, NN)
            score = jnp.where(row >= col, score * scale, LOW)
            top = jnp.max(score, -1, keepdims=True)
            weight = jnp.exp2(score - top)
            m_ref[g] = top
            l_ref[g] = jnp.sum(weight, -1, keepdims=True)
            o_ref[g] = mm(weight.astype(BF16), v_ref[h], NN)


def frames_kernel(x_ref, q_ref, kv_ref, s_ref):
    blocks, _, n, width = x_ref.shape
    before, after = None, None
    for a in range(blocks):
        b = blocks - 1 - a
        query, key = x_ref[a, 0], x_ref[b, 1]
        kv_ref[b * n : b * n + n, width:] = x_ref[b, 2]
        if a == 0:
            q_ref[:n] = query
            kv_ref[b * n : b * n + n, :width] = key
            before, after = x_ref[a, 3], x_ref[b, 3]
        else:
            q_ref[a * n : a * n + n] = fine(query, before, NN)
            kv_ref[b * n : b * n + n, :width] = fine(key, after, NT)
            before, after = fine(x_ref[a, 3], before, NN), fine(after, x_ref[b, 3], NN)
    s_ref[...] = before


def near_attention(x_ref, key_ref, cat_ref, value_ref, store, between):
    blocks, _, n, width = x_ref.shape
    store(0, jnp.zeros((n, width), F32), jnp.full((n, 1), LOW, F32), jnp.zeros((n, 1), F32))
    for a in range(1, blocks):
        last, rows = (a - 1) * n, a * n
        if a > 1:
            key_ref[:last] = mm(cat_ref[:last], left(x_ref[a - 1, 3], 1), NT)
        key_ref[last:rows] = x_ref[a - 1, 1]
        value_ref[last:rows] = x_ref[a - 1, 2].astype(BF16)
        cat_ref[:rows] = right(key_ref[:rows], 1)
        score = mm(left(x_ref[a, 0], 1), cat_ref[:rows], NT)
        top = jnp.max(score, -1, keepdims=True)
        weight = jnp.exp2(score - top)
        store(a, mm(weight.astype(BF16), value_ref[:rows], NN), top, jnp.sum(weight, -1, keepdims=True))
        between(a)


def section_kernel(
    x_ref, q_in, kv_ref, map_ref, out_ref,
    all_kv, maps, frames, partner_q, product, key_ref, cats, values,
    o_ref, m_ref, l_ref, pack, partner_pack,
    local_sem, kv_send, kv_recv, map_send, map_recv, q_sems, pack_send, pack_recv,
):
    blocks, _, n, width = x_ref.shape
    rows = blocks * n
    quarter_rows, step = rows // 4, 512
    sections = maps.shape[0]
    chips = sections // 2
    s, k = lax.axis_index("sec"), lax.axis_index("key")
    x, c = s // 2, s % 2
    z = k % 4
    sibling, partner = s + 1 - 2 * c, sections - 1 - s
    helper = s < sections // 2
    ahead_chip, behind_chip, across_chip = (x + 1) % chips, (x + chips - 1) % chips, (x + 2) % chips
    ahead, behind, across = (chip * 2 + c for chip in (ahead_chip, behind_chip, across_chip))
    z_next, z_last = k - z + (z + 1) % 4, k - z + (z + 3) % 4
    mine, other = z % 2 * 2, 2 - z % 2 * 2
    mesh_ids = pl.DeviceIdType.MESH

    def need(t, chip):
        return (
            ((chip == 0) & (t == 2))
            | ((chip == 1) & (t < 2))
            | ((chip == 2) & ((t < 2) | (t == 3)))
            | ((chip == 3) & (t >= 3) & (t <= 5))
        )

    def place(t, quarter):
        return all_kv.at[t % 6, pl.ds(pl.multiple_of(quarter * quarter_rows, quarter_rows), quarter_rows)]

    sent = []

    def put(when, t, quarter, device, source=None):
        copy = pltpu.make_async_remote_copy(
            src_ref=place(t, quarter) if source is None else source,
            dst_ref=place(t, quarter),
            send_sem=kv_send.at[len(sent)],
            recv_sem=kv_recv.at[t, quarter],
            device_id=device,
            device_id_type=mesh_ids,
        )
        pl.when(when)(copy.start)
        sent.append((when, copy))

    def got(when, t, quarter):
        copy = pltpu.make_async_remote_copy(
            src_ref=place(t, quarter),
            dst_ref=place(t, quarter),
            send_sem=kv_send.at[0],
            recv_sem=kv_recv.at[t, quarter],
            device_id=(sibling, k),
            device_id_type=mesh_ids,
        )
        pl.when(when)(copy.wait_recv)

    others = [(s + d) % sections for d in range(1, sections)]
    barrier = pltpu.get_barrier_semaphore()
    greeted = [(t, k) for t in others] + [(s, z_next), (s, z_last)]
    for device in greeted:
        pl.semaphore_signal(barrier, inc=1, device_id=device, device_id_type=mesh_ids)
    pl.semaphore_wait(barrier, len(greeted))

    map_copies = [
        pltpu.make_async_remote_copy(
            src_ref=map_ref,
            dst_ref=maps.at[s],
            send_sem=map_send.at[d],
            recv_sem=map_recv.at[s],
            device_id=(t, k),
            device_id_type=mesh_ids,
        )
        for d, t in enumerate(others)
    ]
    for copy in map_copies:
        copy.start()
    own_copy = pltpu.make_async_copy(kv_ref, all_kv.at[s % 6], local_sem)
    pl.when(helper)(own_copy.start)
    for index in range(2):
        source = kv_ref.at[pl.ds(pl.multiple_of((mine + index) * quarter_rows, quarter_rows), quarter_rows)]
        onward = need(s, across_chip)
        put(need(s, ahead_chip) | (onward & (index == 0)), s, mine + index, (ahead, k), source)
        put(need(s, behind_chip) | (onward & (index == 1)), s, mine + index, (behind, k), source)
    query_copy = pltpu.make_async_remote_copy(
        src_ref=q_in,
        dst_ref=partner_q,
        send_sem=q_sems.at[0],
        recv_sem=q_sems.at[1],
        device_id=(partner, k),
        device_id_type=mesh_ids,
    )
    pl.when(jnp.logical_not(helper))(query_copy.start)
    for quarter in range(4):
        source = kv_ref.at[quarter * quarter_rows : (quarter + 1) * quarter_rows]
        put(s != sections - 1, s, quarter, (sibling, k), source)

    def pass_mine(t, index, onward, onward_when):
        here = need(t, x)
        got(here | onward_when, t, mine + index)
        if onward is not None:
            put(onward_when, t, mine + index, (onward, k))
        put(here, t, mine + index, (s, z_last if index else z_next))
        put(here, t, mine + index, (sibling, k))

    def pass_other(t, index):
        got(need(t, x), t, other + index)
        put(need(t, x), t, other + index, (sibling, k))

    def between(a):
        if a == 9:
            pass_mine(behind, 0, ahead, need(behind, ahead_chip))
            pass_mine(ahead, 0, None, False)
        if a == 13:
            pass_mine(behind, 1, None, False)
            pass_mine(ahead, 1, behind, need(ahead, behind_chip))

    def store(a, o, m, l):
        at = slice(a * n, a * n + n)
        o_ref[at], m_ref[at], l_ref[at] = o, m, l

    near_attention(x_ref, key_ref, cats.at[0], values.at[0], store, between)
    o_ref[rows:] = jnp.zeros((rows, width), F32)
    m_ref[rows:] = jnp.full((rows, 1), LOW, F32)
    l_ref[rows:] = jnp.zeros((rows, 1), F32)

    maps[s] = map_ref[...]
    for d, t in enumerate(others):
        map_copies[d].wait_send()
        pltpu.make_async_remote_copy(
            src_ref=map_ref,
            dst_ref=maps.at[t],
            send_sem=map_send.at[d],
            recv_sem=map_recv.at[t],
            device_id=(t, k),
            device_id_type=mesh_ids,
        ).wait_recv()

    def helped(owner, t):
        return ((owner >= 6) & (t <= 2)) | (((owner == 4) | (owner == 5)) & (t == 2))

    def own_slot(t):
        return t - jnp.where(s >= 6, 3, jnp.where((s >= 4) & (t > 2), 1, 0))

    def helper_slot(t):
        return jnp.where(s < 2, s + t, s)

    def build(q_ref, count, wanted, slot):
        def turn(index, carry):
            t = count - 1 - index

            @pl.when(wanted(t) & (index == 0))
            def _():
                frames[slot(t)] = left(q_ref[...], 1)

            @pl.when(wanted(t) & (index > 0))
            def _():
                frames[slot(t)] = left(fine(q_ref[...], product[...], NN), 1)

            @pl.when((index == 0) & (t > 0))
            def _():
                product[...] = maps[t]

            @pl.when((index > 0) & (t > 0))
            def _():
                product[...] = fine(product[...], maps[t], NN)

            return carry

        lax.fori_loop(0, count, turn, 0)

    build(q_in, s, lambda t: jnp.logical_not(helped(s, t)), own_slot)

    @pl.when(helper)
    def _():
        query_copy.wait_recv()
        build(partner_q, partner, lambda t: helped(partner, t), helper_slot)

    for index in range(2):
        pass_other(behind, index)
        pass_other(ahead, index)
    pass_mine(across, 0, None, False)
    pass_mine(across, 1, None, False)
    for quarter in range(4):
        got(sibling != sections - 1, sibling, quarter)

    def attend_rows(query, here, slot):
        score = mm(query, cats[slot], NT)
        old = m_ref[here, :]
        top = jnp.maximum(old, jnp.max(score, -1, keepdims=True))
        weight = jnp.exp2(score - top)
        factor = jnp.exp2(old - top)
        m_ref[here, :] = top
        l_ref[here, :] = l_ref[here, :] * factor + jnp.sum(weight, -1, keepdims=True)
        o_ref[here, :] = o_ref[here, :] * factor + mm(weight.astype(BF16), values[slot], NN)

    def convert(t, slot):
        cats[slot] = right(all_kv[t % 6, :, :width], 1)
        values[slot] = all_kv[t % 6, :, width:].astype(BF16)

    row, col = grids(n)
    eye = row == col
    part_blocks = step // n

    def packed(target, a, o, m, l):
        target[a, :n] = o
        target[a, n : n + 1] = as_row(m, eye)
        target[a, n + 1 : n + 2] = as_row(l, eye)
        target[a, n + 2 :] = jnp.zeros((WIDE - 2, width), F32)

    def pack_copy(at):
        piece = pl.ds(at * part_blocks, part_blocks)
        return pltpu.make_async_remote_copy(
            src_ref=pack.at[piece],
            dst_ref=partner_pack.at[piece],
            send_sem=pack_send.at[at],
            recv_sem=pack_recv.at[at],
            device_id=(partner, k),
            device_id_type=mesh_ids,
        )

    @pl.when(helper)
    def _():
        own_copy.wait()
        first_slot = s < 2
        for quarter in range(4):
            got(s == 1, 2, quarter)
        count = jnp.where(first_slot, 3, 1)

        def prepare(index, carry):
            convert(jnp.where(first_slot, index, 2), index)
            return carry

        lax.fori_loop(0, count, prepare, 0)

        def rows_part(at, carry):
            here = pl.ds(pl.multiple_of(rows + at * step, step), step)

            def one(index, carry):
                frame = helper_slot(jnp.where(first_slot, index, 2))
                attend_rows(frames[frame, pl.ds(pl.multiple_of(at * step, step), step), :], here, index)
                return carry

            lax.fori_loop(0, count, one, 0)
            for block in range(part_blocks):
                these = pl.ds(pl.multiple_of(rows + at * step + block * n, n), n)
                packed(pack, at * part_blocks + block, o_ref[these, :], m_ref[these, :], l_ref[these, :])
            pack_copy(at).start()
            return carry

        lax.fori_loop(0, rows // step, rows_part, 0)

    def tile(t):
        @pl.when((t < s) & jnp.logical_not(helped(s, t)))
        def _():
            convert(t, 0)

            def part(at, carry):
                here = pl.ds(pl.multiple_of(at * step, step), step)
                attend_rows(frames[own_slot(t), here, :], here, 0)
                return carry

            lax.fori_loop(0, rows // step, part, 0)

    beside_behind, beside_across = behind + 1 - 2 * c, across + 1 - 2 * c
    tile(sibling)
    pass_other(across, 0)
    pass_other(across, 1)
    tile(behind)
    for quarter in range(4):
        got(need(beside_behind, x), beside_behind, quarter)
    tile(beside_behind)
    tile(across)
    for quarter in range(4):
        got(need(beside_across, x), beside_across, quarter)
    tile(beside_across)

    @pl.when(helper)
    def _():
        def finish(a, carry):
            here = pl.ds(pl.multiple_of(a * n, n), n)
            packed(out_ref, a, o_ref[here, :], m_ref[here, :], l_ref[here, :])
            return carry

        lax.fori_loop(0, blocks, finish, 0)
        for at in range(rows // step):
            pack_copy(at).wait_send()

    @pl.when(jnp.logical_not(helper))
    def _():
        query_copy.wait_send()

        def finish(at, carry):
            pack_copy(at).wait_recv()
            for block in range(part_blocks):
                a = at * part_blocks + block
                here = pl.ds(pl.multiple_of(a * n, n), n)
                far_top = as_column(partner_pack[a, n : n + 1], eye)
                far_sum = as_column(partner_pack[a, n + 1 : n + 2], eye)
                near_top = m_ref[here, :]
                top = jnp.maximum(far_top, near_top)
                far_factor, factor = jnp.exp2(far_top - top), jnp.exp2(near_top - top)
                o = partner_pack[a, :n] * far_factor + o_ref[here, :] * factor
                packed(out_ref, a, o, top, far_sum * far_factor + l_ref[here, :] * factor)
            return carry

        lax.fori_loop(0, rows // step, finish, 0)

    for when, copy in sent:
        pl.when(when)(copy.wait_send)


def merge_kernel(far_ref, o_ref, m_ref, l_ref, out_ref):
    heads, n, width = o_ref.shape
    row, col = grids(n)
    for g in range(heads):
        far_top = as_column(far_ref[g, n : n + 1], row == col)
        far_sum = as_column(far_ref[g, n + 1 : n + 2], row == col)
        near_top = m_ref[g]
        top = jnp.maximum(far_top, near_top)
        far_factor, near_factor = jnp.exp2(far_top - top), jnp.exp2(near_top - top)
        total = far_sum * far_factor + l_ref[g] * near_factor
        mixed = far_ref[g, :n] * far_factor + o_ref[g] * near_factor
        out_ref[g] = (mixed / total).astype(BF16)


def shape(*dims, dtype=F32):
    return jax.ShapeDtypeStruct(dims, dtype)


def call(kernel, out_shape, *operands, scratch=(), in_specs=None, **params):
    return pl.pallas_call(
        kernel,
        out_shape=out_shape,
        in_specs=in_specs or [pl.BlockSpec(memory_space=pltpu.VMEM)] * len(operands),
        out_specs=jax.tree.map(lambda _: pl.BlockSpec(memory_space=pltpu.VMEM), out_shape),
        scratch_shapes=list(scratch),
        compiler_params=pltpu.CompilerParams(vmem_limit_bytes=VMEM_LIMIT, **params),
    )(*operands)


def body(query, key, value, raw_directions, beta_raw_logits):
    n, heads, width = query.shape
    kv_heads = key.shape[1]
    blocks = lax.axis_size("key")
    sections = lax.axis_size("sec")
    rows = n * blocks
    scale = width ** (-0.5) * math.log2(math.e)
    q, k, v, w = (jnp.transpose(x, (1, 0, 2)) for x in (query, key, value, raw_directions))
    sent, z, qw = call(
        functools.partial(terms_kernel, scale),
        [shape(heads, 4, n, width), shape(kv_heads, n, n), shape(heads, n, n)],
        q, k, v, w, beta_raw_logits,
    )
    near = lax.all_to_all(sent, "key", split_axis=0, concat_axis=0, tiled=True)
    own = call(
        functools.partial(diagonal_kernel, scale),
        [shape(heads, n, width), shape(heads, n, 1), shape(heads, n, 1)],
        q, k, v, z, qw,
    )
    section_query, section_kv, section_map = call(
        frames_kernel, [shape(rows, width), shape(rows, 2 * width), shape(width, width)], near
    )
    vmem, dma = pltpu.VMEM, pltpu.SemaphoreType.DMA
    back = call(
        section_kernel,
        shape(blocks, n + WIDE, width),
        near, section_query, section_kv, section_map,
        scratch=[
            vmem((6, rows, 2 * width), F32),
            vmem((sections, width, width), F32),
            vmem((4, rows, 4 * width), BF16),
            vmem((rows, width), F32),
            vmem((width, width), F32),
            vmem((rows, width), F32),
            vmem((3, rows, 4 * width), BF16),
            vmem((3, rows, width), BF16),
            vmem((2 * rows, width), F32),
            vmem((2 * rows, 1), F32),
            vmem((2 * rows, 1), F32),
            vmem((blocks, n + WIDE, width), F32),
            vmem((blocks, n + WIDE, width), F32),
            dma,
            dma((28,)),
            dma((sections, 4)),
            dma((sections - 1,)),
            dma((sections,)),
            dma((2,)),
            dma((4,)),
            dma((4,)),
        ],
        collective_id=0,
        has_side_effects=True,
    )
    far = lax.all_to_all(back, "key", split_axis=0, concat_axis=0, tiled=True)
    merged = call(merge_kernel, shape(heads, n, width, dtype=BF16), far, *own)
    return jnp.transpose(merged, (1, 0, 2))


def solution(mesh):
    spec = P(("sec", "key"), None, None)
    return jax.shard_map(
        body,
        mesh=mesh,
        in_specs=(spec, spec, spec, spec, P(("sec", "key"), None)),
        out_specs=spec,
        check_vma=False,
    )
```

```python
import functools
import math

import jax
import jax.numpy as jnp
from jax import lax
from jax.experimental import pallas as pl
from jax.experimental.pallas import tpu as pltpu
from jax.sharding import PartitionSpec as P

F32 = jnp.float32
BF16 = jnp.bfloat16
NN = ((1,), (0,))
NT = ((1,), (1,))
TN = ((0,), (0,))
LOW = -1e30
VMEM_LIMIT = 56 * 1024 * 1024
WIDE = 8


def halves(x):
    high = x.astype(BF16)
    return high, (x - high.astype(F32)).astype(BF16)


def left(x, axis):
    high, low = halves(x)
    return jnp.concatenate([high, low, high, low], axis)


def right(x, axis):
    high, low = halves(x)
    return jnp.concatenate([high, high, low, low], axis)


def mm(a, b, dims):
    return lax.dot_general(a, b, (dims, ((), ())), preferred_element_type=F32)


def fine(a, b, dims):
    return mm(left(a, dims[0][0]), right(b, dims[1][0]), dims)


def grids(n):
    return lax.broadcasted_iota(jnp.int32, (n, n), 0), lax.broadcasted_iota(jnp.int32, (n, n), 1)


def as_row(column, eye):
    return jnp.sum(jnp.where(eye, column, 0.0), 0, keepdims=True)


def as_column(row, eye):
    return jnp.sum(jnp.where(eye, row, 0.0), 1, keepdims=True)


def exchange_kernel(
    scale, q_ref, k_ref, v_ref, w_ref, b_ref,
    near_ref, z_ref, qw_ref, qs_ref, kvs_ref, map_ref,
    shared, starts, send_sems, recv_sems,
):
    blocks = near_ref.shape[0]
    section, me = lax.axis_index("sec"), lax.axis_index("key")
    mesh_ids = pl.DeviceIdType.MESH
    barrier = pltpu.get_barrier_semaphore()

    def greet(d, carry):
        device = (section, (me + d) % blocks)
        pl.semaphore_signal(barrier, inc=1, device_id=device, device_id_type=mesh_ids)
        return carry

    lax.fori_loop(1, blocks, greet, 0)
    pl.semaphore_wait(barrier, blocks - 1)
    heads, n, width = k_ref.shape
    group = q_ref.shape[0] // heads
    row, col = grids(n)

    def outgoing(to, piece):
        return pltpu.make_async_remote_copy(
            src_ref=starts.at[to] if piece == 0 else shared.at[to // group, piece - 1],
            dst_ref=near_ref.at[me, piece],
            send_sem=send_sems.at[to, piece],
            recv_sem=recv_sems.at[me, piece],
            device_id=(section, to),
            device_id_type=mesh_ids,
        )

    def send(piece):
        def one(d, carry):
            outgoing((me + d) % blocks, piece).start()
            return carry

        lax.fori_loop(1, blocks, one, 0)

    def arrive(piece):
        def one(d, carry):
            source = (me + d) % blocks
            outgoing(source, piece).wait_send()
            pltpu.make_async_remote_copy(
                src_ref=starts.at[source],
                dst_ref=near_ref.at[source, piece],
                send_sem=send_sems.at[source, piece],
                recv_sem=recv_sems.at[source, piece],
                device_id=(section, source),
                device_id_type=mesh_ids,
            ).wait_recv()
            return carry

        lax.fori_loop(1, blocks, one, 0)

    for h in range(heads):
        shared[h, 1] = v_ref[h].astype(F32)
    near_ref[me, 2] = shared[me // group, 1]
    send(2)
    units, betas, lows, inverses = [], [], [], []
    for h in range(heads):
        w = w_ref[h].astype(F32)
        unit = w / jnp.sqrt(jnp.sum(w * w, -1, keepdims=True) + 1e-6)
        beta = 2.0 / (1.0 + jnp.exp(-b_ref[:, h : h + 1]))
        low = jnp.where(row > col, beta * fine(unit, unit, NT), 0.0)
        first = ((row ^ col) == 1) & (row > col)
        units.append(unit)
        betas.append(beta)
        lows.append(low)
        inverses.append(jnp.where(row == col, 1.0, jnp.where(first, -low, 0.0)))
    size = 2
    while size < n:
        pick = ((row ^ col) < 2 * size) & ((row & size) != 0) & ((col & size) == 0)
        inner = [fine(jnp.where(pick, lows[h], 0.0), inverses[h], NN) for h in range(heads)]
        inverses = [inverses[h] - fine(inverses[h], inner[h], NN) for h in range(heads)]
        size *= 2
    ys, sides = [], []
    for h in range(heads):
        unit, beta, inverse = units[h], betas[h], inverses[h]
        key = k_ref[h]
        high, low = halves(unit)
        both = jnp.concatenate([high, low], 1)
        cross = jnp.where(row > col, mm(both, jnp.concatenate([key, key], 1), NT), 0.0)
        solved = fine(inverse, jnp.concatenate([beta * unit, beta * cross], 1), NN)
        y, z = solved[:, :width], solved[:, width:]
        z_ref[h] = z
        ys.append(right(y, 0))
        sides.append(both)
        shared[h, 2] = jnp.where(row == col, 1.0, 0.0) - fine(unit, y, TN)
        shared[h, 0] = key.astype(F32) - fine(z, unit, TN)
    near_ref[me, 3] = shared[me // group, 2]
    near_ref[me, 1] = shared[me // group, 0]
    send(3)
    send(1)
    for h in range(heads):
        for g in range(h * group, h * group + group):
            query = q_ref[g]
            qw = jnp.where(row >= col, mm(jnp.concatenate([query, query], 1), sides[h], NT), 0.0)
            qw_ref[g] = qw
            starts[g] = (query.astype(F32) - mm(left(qw, 1), ys[h], NN)) * scale
    near_ref[me, 0] = starts[me]
    send(0)

    arrive(3)
    pairs = [fine(near_ref[2 * g + 1, 3], near_ref[2 * g, 3], NN) for g in range(blocks // 2)]
    before, after = [None], [None] * blocks
    reach = None
    for g in range(blocks // 2):
        even, b = near_ref[2 * g, 3], blocks // 2 - 1 - g
        before.append(even if g == 0 else fine(even, before[2 * g], NN))
        before.append(pairs[g] if g == 0 else fine(pairs[g], before[2 * g], NN))
        after[2 * b + 1] = reach
        odd = near_ref[2 * b + 1, 3]
        after[2 * b] = odd if g == 0 else fine(reach, odd, NN)
        reach = pairs[b] if g == 0 else fine(reach, pairs[b], NN)
    map_ref[...] = before[blocks]
    arrive(1)
    for b in range(blocks):
        key = near_ref[b, 1]
        kvs_ref[b * n : b * n + n, :width] = key if after[b] is None else fine(key, after[b], NT)
    arrive(2)
    for b in range(blocks):
        kvs_ref[b * n : b * n + n, width:] = near_ref[b, 2]
    arrive(0)
    for a in range(blocks):
        query = near_ref[a, 0]
        qs_ref[a * n : a * n + n] = query if a == 0 else fine(query, before[a], NN)


def diagonal_kernel(scale, q_ref, k_ref, v_ref, z_ref, qw_ref, o_ref, m_ref, l_ref):
    heads, n, width = k_ref.shape
    group = q_ref.shape[0] // heads
    row, col = grids(n)
    for h in range(heads):
        z_right = right(z_ref[h], 0)
        for g in range(h * group, h * group + group):
            score = mm(q_ref[g], k_ref[h], NT) - mm(left(qw_ref[g], 1), z_right, NN)
            score = jnp.where(row >= col, score * scale, LOW)
            top = jnp.max(score, -1, keepdims=True)
            weight = jnp.exp2(score - top)
            m_ref[g] = top
            l_ref[g] = jnp.sum(weight, -1, keepdims=True)
            o_ref[g] = mm(weight.astype(BF16), v_ref[h], NN)


def near_attention(x_ref, key_ref, cat_ref, value_ref, store):
    blocks, _, n, width = x_ref.shape
    pair = 2 * n
    for g in range(blocks // 2):
        first, second, past = 2 * g, 2 * g + 1, g * pair
        if g > 0:
            old = past - pair
            if g > 1:
                both = fine(x_ref[first - 1, 3], x_ref[first - 2, 3], NN)
                key_ref[:old] = mm(cat_ref[:old], left(both, 1), NT)
            key_ref[old : old + n] = fine(x_ref[first - 2, 1], x_ref[first - 1, 3], NT)
            key_ref[old + n : past] = x_ref[first - 1, 1]
            value_ref[old : old + n] = x_ref[first - 2, 2].astype(BF16)
            value_ref[old + n : past] = x_ref[first - 1, 2].astype(BF16)
            cat_ref[:past] = right(key_ref[:past], 1)
        later = x_ref[second, 0]
        inner = fine(later, x_ref[first, 1], NT)
        inner_value = x_ref[first, 2].astype(BF16)
        inner_top = jnp.max(inner, -1, keepdims=True)
        if g == 0:
            weight = jnp.exp2(inner - inner_top)
            store(0, jnp.zeros((n, width), F32), jnp.full((n, 1), LOW, F32), jnp.zeros((n, 1), F32))
            o = mm(weight.astype(BF16), inner_value, NN)
            store(1, o, inner_top, jnp.sum(weight, -1, keepdims=True))
            continue
        query = jnp.concatenate([x_ref[first, 0], fine(later, x_ref[first, 3], NN)], 0)
        score = mm(left(query, 1), cat_ref[:past], NT)
        top = jnp.max(score, -1, keepdims=True)
        top = jnp.concatenate([top[:n], jnp.maximum(top[n:], inner_top)], 0)
        weight = jnp.exp2(score - top)
        inner_weight = jnp.exp2(inner - top[n:])
        total = jnp.sum(weight, -1, keepdims=True)
        o = mm(weight.astype(BF16), value_ref[:past], NN)
        store(first, o[:n], top[:n], total[:n])
        inner_o = mm(inner_weight.astype(BF16), inner_value, NN)
        store(second, o[n:] + inner_o, top[n:], total[n:] + jnp.sum(inner_weight, -1, keepdims=True))


def section_kernel(
    x_ref, q_in, kv_ref, map_ref, out_ref,
    all_kv, maps, frames, partner_q, product, key_ref, cats, values,
    o_ref, m_ref, l_ref, pack, partner_pack,
    local_sem, kv_send, kv_recv, map_send, map_recv, q_sems, pack_send, pack_recv,
):
    blocks, _, n, width = x_ref.shape
    rows = blocks * n
    quarter_rows, step = rows // 4, 512
    sections = maps.shape[0]
    chips = sections // 2
    s, k = lax.axis_index("sec"), lax.axis_index("key")
    x, c = s // 2, s % 2
    z = k % 4
    sibling, partner = s + 1 - 2 * c, sections - 1 - s
    helper = s < sections // 2
    ahead_chip, behind_chip, across_chip = (x + 1) % chips, (x + chips - 1) % chips, (x + 2) % chips
    ahead, behind, across = (chip * 2 + c for chip in (ahead_chip, behind_chip, across_chip))
    z_next, z_last = k - z + (z + 1) % 4, k - z + (z + 3) % 4
    mine, other = z % 2 * 2, 2 - z % 2 * 2
    mesh_ids = pl.DeviceIdType.MESH

    def need(t, chip):
        return (
            ((chip == 0) & (t == 2))
            | ((chip == 1) & (t < 2))
            | ((chip == 2) & ((t < 2) | (t == 3)))
            | ((chip == 3) & (t >= 3) & (t <= 5))
        )

    def place(t, quarter):
        return all_kv.at[t % 6, pl.ds(pl.multiple_of(quarter * quarter_rows, quarter_rows), quarter_rows)]

    sent = []

    def put(when, t, quarter, device, source=None):
        copy = pltpu.make_async_remote_copy(
            src_ref=place(t, quarter) if source is None else source,
            dst_ref=place(t, quarter),
            send_sem=kv_send.at[len(sent)],
            recv_sem=kv_recv.at[t, quarter],
            device_id=device,
            device_id_type=mesh_ids,
        )
        pl.when(when)(copy.start)
        sent.append((when, copy))

    def got(when, t, quarter):
        copy = pltpu.make_async_remote_copy(
            src_ref=place(t, quarter),
            dst_ref=place(t, quarter),
            send_sem=kv_send.at[0],
            recv_sem=kv_recv.at[t, quarter],
            device_id=(sibling, k),
            device_id_type=mesh_ids,
        )
        pl.when(when)(copy.wait_recv)

    others = [(s + d) % sections for d in range(1, sections)]
    barrier = pltpu.get_barrier_semaphore()
    greeted = [(t, k) for t in others] + [(s, z_next), (s, z_last)]
    for device in greeted:
        pl.semaphore_signal(barrier, inc=1, device_id=device, device_id_type=mesh_ids)
    pl.semaphore_wait(barrier, len(greeted))

    map_copies = [
        pltpu.make_async_remote_copy(
            src_ref=map_ref,
            dst_ref=maps.at[s],
            send_sem=map_send.at[d],
            recv_sem=map_recv.at[s],
            device_id=(t, k),
            device_id_type=mesh_ids,
        )
        for d, t in enumerate(others)
    ]
    for copy in map_copies:
        copy.start()
    own_copy = pltpu.make_async_copy(kv_ref, all_kv.at[s % 6], local_sem)
    pl.when(helper)(own_copy.start)
    for index in range(2):
        source = kv_ref.at[pl.ds(pl.multiple_of((mine + index) * quarter_rows, quarter_rows), quarter_rows)]
        onward = need(s, across_chip)
        put(need(s, ahead_chip) | (onward & (index == 0)), s, mine + index, (ahead, k), source)
        put(need(s, behind_chip) | (onward & (index == 1)), s, mine + index, (behind, k), source)
    query_copy = pltpu.make_async_remote_copy(
        src_ref=q_in,
        dst_ref=partner_q,
        send_sem=q_sems.at[0],
        recv_sem=q_sems.at[1],
        device_id=(partner, k),
        device_id_type=mesh_ids,
    )
    pl.when(jnp.logical_not(helper))(query_copy.start)
    for quarter in range(4):
        source = kv_ref.at[quarter * quarter_rows : (quarter + 1) * quarter_rows]
        put(s != sections - 1, s, quarter, (sibling, k), source)

    def pass_mine(t, index, onward, onward_when):
        here = need(t, x)
        got(here | onward_when, t, mine + index)
        if onward is not None:
            put(onward_when, t, mine + index, (onward, k))
        put(here, t, mine + index, (s, z_last if index else z_next))
        put(here, t, mine + index, (sibling, k))

    def pass_other(t, index):
        got(need(t, x), t, other + index)
        put(need(t, x), t, other + index, (sibling, k))

    def store(a, o, m, l):
        at = slice(a * n, a * n + n)
        o_ref[at], m_ref[at], l_ref[at] = o, m, l

    near_attention(x_ref, key_ref, cats.at[0], values.at[0], store)
    pass_mine(behind, 0, ahead, need(behind, ahead_chip))
    pass_mine(ahead, 0, None, False)
    o_ref[rows:] = jnp.zeros((rows, width), F32)
    m_ref[rows:] = jnp.full((rows, 1), LOW, F32)
    l_ref[rows:] = jnp.zeros((rows, 1), F32)

    maps[s] = map_ref[...]
    for d, t in enumerate(others):
        map_copies[d].wait_send()
        pltpu.make_async_remote_copy(
            src_ref=map_ref,
            dst_ref=maps.at[t],
            send_sem=map_send.at[d],
            recv_sem=map_recv.at[t],
            device_id=(t, k),
            device_id_type=mesh_ids,
        ).wait_recv()

    def helped(owner, t):
        return ((owner >= 6) & (t <= 2)) | (((owner == 4) | (owner == 5)) & (t == 2))

    def own_slot(t):
        return t - jnp.where(s >= 6, 3, jnp.where((s >= 4) & (t > 2), 1, 0))

    def helper_slot(t):
        return jnp.where(s < 2, s + t, s)

    def build(q_ref, count, wanted, slot):
        def turn(index, carry):
            t = count - 1 - index

            @pl.when(wanted(t) & (index == 0))
            def _():
                frames[slot(t)] = left(q_ref[...], 1)

            @pl.when(wanted(t) & (index > 0))
            def _():
                frames[slot(t)] = left(fine(q_ref[...], product[...], NN), 1)

            @pl.when((index == 0) & (t > 0))
            def _():
                product[...] = maps[t]

            @pl.when((index > 0) & (t > 0))
            def _():
                product[...] = fine(product[...], maps[t], NN)

            return carry

        lax.fori_loop(0, count, turn, 0)

    build(q_in, s, lambda t: jnp.logical_not(helped(s, t)), own_slot)
    pass_mine(behind, 1, None, False)
    pass_mine(ahead, 1, behind, need(ahead, behind_chip))

    @pl.when(helper)
    def _():
        query_copy.wait_recv()
        build(partner_q, partner, lambda t: helped(partner, t), helper_slot)

    for index in range(2):
        pass_other(behind, index)
        pass_other(ahead, index)
    pass_mine(across, 0, None, False)
    pass_mine(across, 1, None, False)
    for quarter in range(4):
        got(sibling != sections - 1, sibling, quarter)

    def attend_rows(query, here, slot):
        score = mm(query, cats[slot], NT)
        old = m_ref[here, :]
        top = jnp.maximum(old, jnp.max(score, -1, keepdims=True))
        weight = jnp.exp2(score - top)
        factor = jnp.exp2(old - top)
        m_ref[here, :] = top
        l_ref[here, :] = l_ref[here, :] * factor + jnp.sum(weight, -1, keepdims=True)
        o_ref[here, :] = o_ref[here, :] * factor + mm(weight.astype(BF16), values[slot], NN)

    def convert(t, slot):
        cats[slot] = right(all_kv[t % 6, :, :width], 1)
        values[slot] = all_kv[t % 6, :, width:].astype(BF16)

    row, col = grids(n)
    eye = row == col
    part_blocks = step // n

    def packed(target, a, o, m, l):
        target[a, :n] = o
        target[a, n : n + 1] = as_row(m, eye)
        target[a, n + 1 : n + 2] = as_row(l, eye)
        target[a, n + 2 :] = jnp.zeros((WIDE - 2, width), F32)

    def pack_copy(at):
        piece = pl.ds(at * part_blocks, part_blocks)
        return pltpu.make_async_remote_copy(
            src_ref=pack.at[piece],
            dst_ref=partner_pack.at[piece],
            send_sem=pack_send.at[at],
            recv_sem=pack_recv.at[at],
            device_id=(partner, k),
            device_id_type=mesh_ids,
        )

    @pl.when(helper)
    def _():
        own_copy.wait()
        first_slot = s < 2
        for quarter in range(4):
            got(s == 1, 2, quarter)
        count = jnp.where(first_slot, 3, 1)

        def prepare(index, carry):
            convert(jnp.where(first_slot, index, 2), index)
            return carry

        lax.fori_loop(0, count, prepare, 0)

        def rows_part(at, carry):
            here = pl.ds(pl.multiple_of(rows + at * step, step), step)

            def one(index, carry):
                frame = helper_slot(jnp.where(first_slot, index, 2))
                attend_rows(frames[frame, pl.ds(pl.multiple_of(at * step, step), step), :], here, index)
                return carry

            lax.fori_loop(0, count, one, 0)
            for block in range(part_blocks):
                these = pl.ds(pl.multiple_of(rows + at * step + block * n, n), n)
                packed(pack, at * part_blocks + block, o_ref[these, :], m_ref[these, :], l_ref[these, :])
            pack_copy(at).start()
            return carry

        lax.fori_loop(0, rows // step, rows_part, 0)

    def tile(t):
        @pl.when((t < s) & jnp.logical_not(helped(s, t)))
        def _():
            convert(t, 0)

            def part(at, carry):
                here = pl.ds(pl.multiple_of(at * step, step), step)
                attend_rows(frames[own_slot(t), here, :], here, 0)
                return carry

            lax.fori_loop(0, rows // step, part, 0)

    beside_behind, beside_across = behind + 1 - 2 * c, across + 1 - 2 * c
    tile(sibling)
    pass_other(across, 0)
    pass_other(across, 1)
    tile(behind)
    for quarter in range(4):
        got(need(beside_behind, x), beside_behind, quarter)
    tile(beside_behind)
    tile(across)
    for quarter in range(4):
        got(need(beside_across, x), beside_across, quarter)
    tile(beside_across)

    @pl.when(helper)
    def _():
        def finish(a, carry):
            here = pl.ds(pl.multiple_of(a * n, n), n)
            packed(out_ref, a, o_ref[here, :], m_ref[here, :], l_ref[here, :])
            return carry

        lax.fori_loop(0, blocks, finish, 0)
        for at in range(rows // step):
            pack_copy(at).wait_send()

    @pl.when(jnp.logical_not(helper))
    def _():
        query_copy.wait_send()

        def finish(at, carry):
            pack_copy(at).wait_recv()
            for block in range(part_blocks):
                a = at * part_blocks + block
                here = pl.ds(pl.multiple_of(a * n, n), n)
                far_top = as_column(partner_pack[a, n : n + 1], eye)
                far_sum = as_column(partner_pack[a, n + 1 : n + 2], eye)
                near_top = m_ref[here, :]
                top = jnp.maximum(far_top, near_top)
                far_factor, factor = jnp.exp2(far_top - top), jnp.exp2(near_top - top)
                o = partner_pack[a, :n] * far_factor + o_ref[here, :] * factor
                packed(out_ref, a, o, top, far_sum * far_factor + l_ref[here, :] * factor)
            return carry

        lax.fori_loop(0, rows // step, finish, 0)

    for when, copy in sent:
        pl.when(when)(copy.wait_send)


def merge_kernel(far_ref, o_ref, m_ref, l_ref, out_ref):
    heads, n, width = o_ref.shape
    row, col = grids(n)
    for g in range(heads):
        far_top = as_column(far_ref[g, n : n + 1], row == col)
        far_sum = as_column(far_ref[g, n + 1 : n + 2], row == col)
        near_top = m_ref[g]
        top = jnp.maximum(far_top, near_top)
        far_factor, near_factor = jnp.exp2(far_top - top), jnp.exp2(near_top - top)
        total = far_sum * far_factor + l_ref[g] * near_factor
        mixed = far_ref[g, :n] * far_factor + o_ref[g] * near_factor
        out_ref[g] = (mixed / total).astype(BF16)


def shape(*dims, dtype=F32):
    return jax.ShapeDtypeStruct(dims, dtype)


def call(kernel, out_shape, *operands, scratch=(), in_specs=None, **params):
    return pl.pallas_call(
        kernel,
        out_shape=out_shape,
        in_specs=in_specs or [pl.BlockSpec(memory_space=pltpu.VMEM)] * len(operands),
        out_specs=jax.tree.map(lambda _: pl.BlockSpec(memory_space=pltpu.VMEM), out_shape),
        scratch_shapes=list(scratch),
        compiler_params=pltpu.CompilerParams(vmem_limit_bytes=VMEM_LIMIT, **params),
    )(*operands)


def body(query, key, value, raw_directions, beta_raw_logits):
    n, heads, width = query.shape
    kv_heads = key.shape[1]
    blocks = lax.axis_size("key")
    sections = lax.axis_size("sec")
    rows = n * blocks
    scale = width ** (-0.5) * math.log2(math.e)
    q, k, v, w = (jnp.transpose(x, (1, 0, 2)) for x in (query, key, value, raw_directions))
    vmem, dma = pltpu.VMEM, pltpu.SemaphoreType.DMA
    near, z, qw, section_query, section_kv, section_map = call(
        functools.partial(exchange_kernel, scale),
        [
            shape(blocks, 4, n, width),
            shape(kv_heads, n, n),
            shape(heads, n, n),
            shape(rows, width),
            shape(rows, 2 * width),
            shape(width, width),
        ],
        q, k, v, w, beta_raw_logits,
        scratch=[vmem((kv_heads, 3, n, width), F32), vmem((heads, n, width), F32), dma((blocks, 4)), dma((blocks, 4))],
        collective_id=1,
        has_side_effects=True,
    )
    own = call(
        functools.partial(diagonal_kernel, scale),
        [shape(heads, n, width), shape(heads, n, 1), shape(heads, n, 1)],
        q, k, v, z, qw,
    )
    back = call(
        section_kernel,
        shape(blocks, n + WIDE, width),
        near, section_query, section_kv, section_map,
        scratch=[
            vmem((6, rows, 2 * width), F32),
            vmem((sections, width, width), F32),
            vmem((4, rows, 4 * width), BF16),
            vmem((rows, width), F32),
            vmem((width, width), F32),
            vmem((rows, width), F32),
            vmem((3, rows, 4 * width), BF16),
            vmem((3, rows, width), BF16),
            vmem((2 * rows, width), F32),
            vmem((2 * rows, 1), F32),
            vmem((2 * rows, 1), F32),
            vmem((blocks, n + WIDE, width), F32),
            vmem((blocks, n + WIDE, width), F32),
            dma,
            dma((28,)),
            dma((sections, 4)),
            dma((sections - 1,)),
            dma((sections,)),
            dma((2,)),
            dma((4,)),
            dma((4,)),
        ],
        collective_id=0,
        has_side_effects=True,
    )
    far = lax.all_to_all(back, "key", split_axis=0, concat_axis=0, tiled=True)
    merged = call(merge_kernel, shape(heads, n, width, dtype=BF16), far, *own)
    return jnp.transpose(merged, (1, 0, 2))


def solution(mesh):
    spec = P(("sec", "key"), None, None)
    return jax.shard_map(
        body,
        mesh=mesh,
        in_specs=(spec, spec, spec, spec, P(("sec", "key"), None)),
        out_specs=spec,
        check_vma=False,
    )
```

```python
import functools
import math

import jax
import jax.numpy as jnp
from jax import lax
from jax.experimental import pallas as pl
from jax.experimental.pallas import tpu as pltpu
from jax.sharding import PartitionSpec as P

F32 = jnp.float32
BF16 = jnp.bfloat16
NN = ((1,), (0,))
NT = ((1,), (1,))
TN = ((0,), (0,))
LOW = -1e30
VMEM_LIMIT = 56 * 1024 * 1024
WIDE = 8


def halves(x):
    high = x.astype(BF16)
    return high, (x - high.astype(F32)).astype(BF16)


def left(x, axis):
    high, low = halves(x)
    return jnp.concatenate([high, low, high, low], axis)


def right(x, axis):
    high, low = halves(x)
    return jnp.concatenate([high, high, low, low], axis)


def mm(a, b, dims):
    return lax.dot_general(a, b, (dims, ((), ())), preferred_element_type=F32)


def fine(a, b, dims):
    return mm(left(a, dims[0][0]), right(b, dims[1][0]), dims)


def grids(n):
    return lax.broadcasted_iota(jnp.int32, (n, n), 0), lax.broadcasted_iota(jnp.int32, (n, n), 1)


def as_row(column, eye):
    return jnp.sum(jnp.where(eye, column, 0.0), 0, keepdims=True)


def as_column(row, eye):
    return jnp.sum(jnp.where(eye, row, 0.0), 1, keepdims=True)


def turned(source, target):
    target[...] = jnp.swapaxes(source[...].astype(F32), 0, 1).astype(target.dtype)


def exchange_kernel(
    scale, q_in, k_in, v_in, w_in, b_ref,
    near_ref, z_ref, qw_ref, qs_ref, kvs_ref, map_ref,
    q_ref, k_ref, w_ref, shared, starts, send_sems, recv_sems,
):
    blocks = near_ref.shape[0]
    section, me = lax.axis_index("sec"), lax.axis_index("key")
    mesh_ids = pl.DeviceIdType.MESH
    barrier = pltpu.get_barrier_semaphore()

    def greet(d, carry):
        device = (section, (me + d) % blocks)
        pl.semaphore_signal(barrier, inc=1, device_id=device, device_id_type=mesh_ids)
        return carry

    lax.fori_loop(1, blocks, greet, 0)
    pl.semaphore_wait(barrier, blocks - 1)
    heads, n, width = k_ref.shape
    group = q_ref.shape[0] // heads
    row, col = grids(n)

    def outgoing(to, piece):
        return pltpu.make_async_remote_copy(
            src_ref=starts.at[to] if piece == 0 else shared.at[to // group, piece - 1],
            dst_ref=near_ref.at[me, piece],
            send_sem=send_sems.at[to, piece],
            recv_sem=recv_sems.at[me, piece],
            device_id=(section, to),
            device_id_type=mesh_ids,
        )

    def send(piece):
        def one(d, carry):
            outgoing((me + d) % blocks, piece).start()
            return carry

        lax.fori_loop(1, blocks, one, 0)

    def arrive(piece):
        def one(d, carry):
            source = (me + d) % blocks
            outgoing(source, piece).wait_send()
            pltpu.make_async_remote_copy(
                src_ref=starts.at[source],
                dst_ref=near_ref.at[source, piece],
                send_sem=send_sems.at[source, piece],
                recv_sem=recv_sems.at[source, piece],
                device_id=(section, source),
                device_id_type=mesh_ids,
            ).wait_recv()
            return carry

        lax.fori_loop(1, blocks, one, 0)

    shared[:, 1] = jnp.swapaxes(v_in[...].astype(F32), 0, 1)
    near_ref[me, 2] = shared[me // group, 1]
    send(2)
    turned(q_in, q_ref)
    turned(k_in, k_ref)
    turned(w_in, w_ref)
    units, betas, lows, inverses = [], [], [], []
    for h in range(heads):
        w = w_ref[h].astype(F32)
        unit = w / jnp.sqrt(jnp.sum(w * w, -1, keepdims=True) + 1e-6)
        beta = 2.0 / (1.0 + jnp.exp(-b_ref[:, h : h + 1]))
        low = jnp.where(row > col, beta * fine(unit, unit, NT), 0.0)
        first = ((row ^ col) == 1) & (row > col)
        units.append(unit)
        betas.append(beta)
        lows.append(low)
        inverses.append(jnp.where(row == col, 1.0, jnp.where(first, -low, 0.0)))
    size = 2
    while size < n:
        pick = ((row ^ col) < 2 * size) & ((row & size) != 0) & ((col & size) == 0)
        inner = [fine(jnp.where(pick, lows[h], 0.0), inverses[h], NN) for h in range(heads)]
        inverses = [inverses[h] - fine(inverses[h], inner[h], NN) for h in range(heads)]
        size *= 2
    ys, sides = [], []
    for h in range(heads):
        unit, beta, inverse = units[h], betas[h], inverses[h]
        key = k_ref[h]
        high, low = halves(unit)
        both = jnp.concatenate([high, low], 1)
        cross = jnp.where(row > col, mm(both, jnp.concatenate([key, key], 1), NT), 0.0)
        solved = fine(inverse, jnp.concatenate([beta * unit, beta * cross], 1), NN)
        y, z = solved[:, :width], solved[:, width:]
        z_ref[h] = z
        ys.append(right(y, 0))
        sides.append(both)
        shared[h, 2] = jnp.where(row == col, 1.0, 0.0) - fine(unit, y, TN)
        shared[h, 0] = key.astype(F32) - fine(z, unit, TN)
    near_ref[me, 3] = shared[me // group, 2]
    near_ref[me, 1] = shared[me // group, 0]
    send(3)
    send(1)
    for h in range(heads):
        for g in range(h * group, h * group + group):
            query = q_ref[g]
            qw = jnp.where(row >= col, mm(jnp.concatenate([query, query], 1), sides[h], NT), 0.0)
            qw_ref[g] = qw
            starts[g] = (query.astype(F32) - mm(left(qw, 1), ys[h], NN)) * scale
    near_ref[me, 0] = starts[me]
    send(0)

    arrive(3)
    pairs = [fine(near_ref[2 * g + 1, 3], near_ref[2 * g, 3], NN) for g in range(blocks // 2)]
    before, after = [None], [None] * blocks
    reach = None
    for g in range(blocks // 2):
        even, b = near_ref[2 * g, 3], blocks // 2 - 1 - g
        before.append(even if g == 0 else fine(even, before[2 * g], NN))
        before.append(pairs[g] if g == 0 else fine(pairs[g], before[2 * g], NN))
        after[2 * b + 1] = reach
        odd = near_ref[2 * b + 1, 3]
        after[2 * b] = odd if g == 0 else fine(reach, odd, NN)
        reach = pairs[b] if g == 0 else fine(reach, pairs[b], NN)
    map_ref[...] = before[blocks]
    arrive(1)
    for b in range(blocks):
        key = near_ref[b, 1]
        kvs_ref[b * n : b * n + n, :width] = key if after[b] is None else fine(key, after[b], NT)
    arrive(2)
    for b in range(blocks):
        kvs_ref[b * n : b * n + n, width:] = near_ref[b, 2]
    arrive(0)
    for a in range(blocks):
        query = near_ref[a, 0]
        qs_ref[a * n : a * n + n] = query if a == 0 else fine(query, before[a], NN)


def diagonal_kernel(scale, q_in, k_in, v_in, z_ref, qw_ref, o_ref, m_ref, l_ref, q_ref, k_ref, v_ref):
    heads, n, width = k_ref.shape
    turned(q_in, q_ref)
    turned(k_in, k_ref)
    turned(v_in, v_ref)
    group = q_ref.shape[0] // heads
    row, col = grids(n)
    for h in range(heads):
        z_right = right(z_ref[h], 0)
        for g in range(h * group, h * group + group):
            score = mm(q_ref[g], k_ref[h], NT) - mm(left(qw_ref[g], 1), z_right, NN)
            score = jnp.where(row >= col, score * scale, LOW)
            top = jnp.max(score, -1, keepdims=True)
            weight = jnp.exp2(score - top)
            m_ref[g] = top
            l_ref[g] = jnp.sum(weight, -1, keepdims=True)
            o_ref[g] = mm(weight.astype(BF16), v_ref[h], NN)


def near_attention(x_ref, key_ref, cat_ref, value_ref, store):
    blocks, _, n, width = x_ref.shape
    pair = 2 * n
    for g in range(blocks // 2):
        first, second, past = 2 * g, 2 * g + 1, g * pair
        if g > 0:
            old = past - pair
            if g > 1:
                both = fine(x_ref[first - 1, 3], x_ref[first - 2, 3], NN)
                key_ref[:old] = mm(cat_ref[:old], left(both, 1), NT)
            key_ref[old : old + n] = fine(x_ref[first - 2, 1], x_ref[first - 1, 3], NT)
            key_ref[old + n : past] = x_ref[first - 1, 1]
            value_ref[old : old + n] = x_ref[first - 2, 2].astype(BF16)
            value_ref[old + n : past] = x_ref[first - 1, 2].astype(BF16)
            cat_ref[:past] = right(key_ref[:past], 1)
        later = x_ref[second, 0]
        inner = fine(later, x_ref[first, 1], NT)
        inner_value = x_ref[first, 2].astype(BF16)
        inner_top = jnp.max(inner, -1, keepdims=True)
        if g == 0:
            weight = jnp.exp2(inner - inner_top)
            store(0, jnp.zeros((n, width), F32), jnp.full((n, 1), LOW, F32), jnp.zeros((n, 1), F32))
            o = mm(weight.astype(BF16), inner_value, NN)
            store(1, o, inner_top, jnp.sum(weight, -1, keepdims=True))
            continue
        query = jnp.concatenate([x_ref[first, 0], fine(later, x_ref[first, 3], NN)], 0)
        score = mm(left(query, 1), cat_ref[:past], NT)
        top = jnp.max(score, -1, keepdims=True)
        top = jnp.concatenate([top[:n], jnp.maximum(top[n:], inner_top)], 0)
        weight = jnp.exp2(score - top)
        inner_weight = jnp.exp2(inner - top[n:])
        total = jnp.sum(weight, -1, keepdims=True)
        o = mm(weight.astype(BF16), value_ref[:past], NN)
        store(first, o[:n], top[:n], total[:n])
        inner_o = mm(inner_weight.astype(BF16), inner_value, NN)
        store(second, o[n:] + inner_o, top[n:], total[n:] + jnp.sum(inner_weight, -1, keepdims=True))


def section_kernel(
    x_ref, q_in, kv_ref, map_ref, out_ref,
    all_kv, maps, frames, partner_q, product, key_ref, cats, values,
    o_ref, m_ref, l_ref, pack, partner_pack,
    local_sem, kv_send, kv_recv, map_send, map_recv, q_sems, pack_send, pack_recv,
):
    blocks, _, n, width = x_ref.shape
    rows = blocks * n
    quarter_rows, step = rows // 4, 512
    sections = maps.shape[0]
    chips = sections // 2
    s, k = lax.axis_index("sec"), lax.axis_index("key")
    x, c = s // 2, s % 2
    z = k % 4
    sibling, partner = s + 1 - 2 * c, sections - 1 - s
    helper = s < sections // 2
    ahead_chip, behind_chip, across_chip = (x + 1) % chips, (x + chips - 1) % chips, (x + 2) % chips
    ahead, behind, across = (chip * 2 + c for chip in (ahead_chip, behind_chip, across_chip))
    z_next, z_last = k - z + (z + 1) % 4, k - z + (z + 3) % 4
    mine, other = z % 2 * 2, 2 - z % 2 * 2
    mesh_ids = pl.DeviceIdType.MESH

    def need(t, chip):
        return (
            ((chip == 0) & (t == 2))
            | ((chip == 1) & (t < 2))
            | ((chip == 2) & ((t < 2) | (t == 3)))
            | ((chip == 3) & (t >= 3) & (t <= 5))
        )

    def place(t, quarter):
        return all_kv.at[t % 6, pl.ds(pl.multiple_of(quarter * quarter_rows, quarter_rows), quarter_rows)]

    sent = []

    def put(when, t, quarter, device, source=None):
        copy = pltpu.make_async_remote_copy(
            src_ref=place(t, quarter) if source is None else source,
            dst_ref=place(t, quarter),
            send_sem=kv_send.at[len(sent)],
            recv_sem=kv_recv.at[t, quarter],
            device_id=device,
            device_id_type=mesh_ids,
        )
        pl.when(when)(copy.start)
        sent.append((when, copy))

    def got(when, t, quarter):
        copy = pltpu.make_async_remote_copy(
            src_ref=place(t, quarter),
            dst_ref=place(t, quarter),
            send_sem=kv_send.at[0],
            recv_sem=kv_recv.at[t, quarter],
            device_id=(sibling, k),
            device_id_type=mesh_ids,
        )
        pl.when(when)(copy.wait_recv)

    others = [(s + d) % sections for d in range(1, sections)]
    barrier = pltpu.get_barrier_semaphore()
    greeted = [(t, k) for t in others] + [(s, z_next), (s, z_last)]
    for device in greeted:
        pl.semaphore_signal(barrier, inc=1, device_id=device, device_id_type=mesh_ids)
    pl.semaphore_wait(barrier, len(greeted))

    map_copies = [
        pltpu.make_async_remote_copy(
            src_ref=map_ref,
            dst_ref=maps.at[s],
            send_sem=map_send.at[d],
            recv_sem=map_recv.at[s],
            device_id=(t, k),
            device_id_type=mesh_ids,
        )
        for d, t in enumerate(others)
    ]
    for copy in map_copies:
        copy.start()
    own_copy = pltpu.make_async_copy(kv_ref, all_kv.at[s % 6], local_sem)
    pl.when(helper)(own_copy.start)
    for index in range(2):
        source = kv_ref.at[pl.ds(pl.multiple_of((mine + index) * quarter_rows, quarter_rows), quarter_rows)]
        onward = need(s, across_chip)
        put(need(s, ahead_chip) | (onward & (index == 0)), s, mine + index, (ahead, k), source)
        put(need(s, behind_chip) | (onward & (index == 1)), s, mine + index, (behind, k), source)
    query_copy = pltpu.make_async_remote_copy(
        src_ref=q_in,
        dst_ref=partner_q,
        send_sem=q_sems.at[0],
        recv_sem=q_sems.at[1],
        device_id=(partner, k),
        device_id_type=mesh_ids,
    )
    pl.when(jnp.logical_not(helper))(query_copy.start)
    for quarter in range(4):
        source = kv_ref.at[quarter * quarter_rows : (quarter + 1) * quarter_rows]
        put(s != sections - 1, s, quarter, (sibling, k), source)

    def pass_mine(t, index, onward, onward_when):
        here = need(t, x)
        got(here | onward_when, t, mine + index)
        if onward is not None:
            put(onward_when, t, mine + index, (onward, k))
        put(here, t, mine + index, (s, z_last if index else z_next))
        put(here, t, mine + index, (sibling, k))

    def pass_other(t, index):
        got(need(t, x), t, other + index)
        put(need(t, x), t, other + index, (sibling, k))

    def store(a, o, m, l):
        at = slice(a * n, a * n + n)
        o_ref[at], m_ref[at], l_ref[at] = o, m, l

    near_attention(x_ref, key_ref, cats.at[0], values.at[0], store)
    pass_mine(behind, 0, ahead, need(behind, ahead_chip))
    pass_mine(ahead, 0, None, False)
    o_ref[rows:] = jnp.zeros((rows, width), F32)
    m_ref[rows:] = jnp.full((rows, 1), LOW, F32)
    l_ref[rows:] = jnp.zeros((rows, 1), F32)

    maps[s] = map_ref[...]
    for d, t in enumerate(others):
        map_copies[d].wait_send()
        pltpu.make_async_remote_copy(
            src_ref=map_ref,
            dst_ref=maps.at[t],
            send_sem=map_send.at[d],
            recv_sem=map_recv.at[t],
            device_id=(t, k),
            device_id_type=mesh_ids,
        ).wait_recv()

    def helped(owner, t):
        return ((owner >= 6) & (t <= 2)) | (((owner == 4) | (owner == 5)) & (t == 2))

    def own_slot(t):
        return t - jnp.where(s >= 6, 3, jnp.where((s >= 4) & (t > 2), 1, 0))

    def helper_slot(t):
        return jnp.where(s < 2, s + t, s)

    def build(q_ref, count, wanted, slot):
        def turn(index, carry):
            t = count - 1 - index

            @pl.when(wanted(t) & (index == 0))
            def _():
                frames[slot(t)] = left(q_ref[...], 1)

            @pl.when(wanted(t) & (index > 0))
            def _():
                frames[slot(t)] = left(fine(q_ref[...], product[...], NN), 1)

            @pl.when((index == 0) & (t > 0))
            def _():
                product[...] = maps[t]

            @pl.when((index > 0) & (t > 0))
            def _():
                product[...] = fine(product[...], maps[t], NN)

            return carry

        lax.fori_loop(0, count, turn, 0)

    build(q_in, s, lambda t: jnp.logical_not(helped(s, t)), own_slot)
    pass_mine(behind, 1, None, False)
    pass_mine(ahead, 1, behind, need(ahead, behind_chip))

    @pl.when(helper)
    def _():
        query_copy.wait_recv()
        build(partner_q, partner, lambda t: helped(partner, t), helper_slot)

    def attend_rows(query, here, slot):
        score = mm(query, cats[slot], NT)
        old = m_ref[here, :]
        top = jnp.maximum(old, jnp.max(score, -1, keepdims=True))
        weight = jnp.exp2(score - top)
        factor = jnp.exp2(old - top)
        m_ref[here, :] = top
        l_ref[here, :] = l_ref[here, :] * factor + jnp.sum(weight, -1, keepdims=True)
        o_ref[here, :] = o_ref[here, :] * factor + mm(weight.astype(BF16), values[slot], NN)

    def convert(t, slot):
        cats[slot] = right(all_kv[t % 6, :, :width], 1)
        values[slot] = all_kv[t % 6, :, width:].astype(BF16)

    def tile(t):
        @pl.when((t < s) & jnp.logical_not(helped(s, t)))
        def _():
            convert(t, 0)

            def part(at, carry):
                here = pl.ds(pl.multiple_of(at * step, step), step)
                attend_rows(frames[own_slot(t), here, :], here, 0)
                return carry

            lax.fori_loop(0, rows // step, part, 0)

    for quarter in range(4):
        got(sibling != sections - 1, sibling, quarter)
    tile(sibling)
    for index in range(2):
        pass_other(behind, index)
        pass_other(ahead, index)
    pass_mine(across, 0, None, False)
    pass_mine(across, 1, None, False)

    row, col = grids(n)
    eye = row == col
    part_blocks = step // n

    def packed(target, a, o, m, l):
        target[a, :n] = o
        target[a, n : n + 1] = as_row(m, eye)
        target[a, n + 1 : n + 2] = as_row(l, eye)
        target[a, n + 2 :] = jnp.zeros((WIDE - 2, width), F32)

    def pack_copy(at):
        piece = pl.ds(at * part_blocks, part_blocks)
        return pltpu.make_async_remote_copy(
            src_ref=pack.at[piece],
            dst_ref=partner_pack.at[piece],
            send_sem=pack_send.at[at],
            recv_sem=pack_recv.at[at],
            device_id=(partner, k),
            device_id_type=mesh_ids,
        )

    @pl.when(helper)
    def _():
        own_copy.wait()
        first_slot = s < 2
        for quarter in range(4):
            got(s == 1, 2, quarter)
        count = jnp.where(first_slot, 3, 1)

        def prepare(index, carry):
            convert(jnp.where(first_slot, index, 2), index)
            return carry

        lax.fori_loop(0, count, prepare, 0)

        def rows_part(at, carry):
            here = pl.ds(pl.multiple_of(rows + at * step, step), step)

            def one(index, carry):
                frame = helper_slot(jnp.where(first_slot, index, 2))
                attend_rows(frames[frame, pl.ds(pl.multiple_of(at * step, step), step), :], here, index)
                return carry

            lax.fori_loop(0, count, one, 0)
            for block in range(part_blocks):
                these = pl.ds(pl.multiple_of(rows + at * step + block * n, n), n)
                packed(pack, at * part_blocks + block, o_ref[these, :], m_ref[these, :], l_ref[these, :])
            pack_copy(at).start()
            return carry

        lax.fori_loop(0, rows // step, rows_part, 0)

    beside_behind, beside_across = behind + 1 - 2 * c, across + 1 - 2 * c
    pass_other(across, 0)
    pass_other(across, 1)
    tile(behind)
    for quarter in range(4):
        got(need(beside_behind, x), beside_behind, quarter)
    tile(beside_behind)
    tile(across)
    for quarter in range(4):
        got(need(beside_across, x), beside_across, quarter)
    tile(beside_across)

    @pl.when(helper)
    def _():
        def finish(a, carry):
            here = pl.ds(pl.multiple_of(a * n, n), n)
            packed(out_ref, a, o_ref[here, :], m_ref[here, :], l_ref[here, :])
            return carry

        lax.fori_loop(0, blocks, finish, 0)
        for at in range(rows // step):
            pack_copy(at).wait_send()

    @pl.when(jnp.logical_not(helper))
    def _():
        query_copy.wait_send()

        def finish(at, carry):
            pack_copy(at).wait_recv()
            for block in range(part_blocks):
                a = at * part_blocks + block
                here = pl.ds(pl.multiple_of(a * n, n), n)
                far_top = as_column(partner_pack[a, n : n + 1], eye)
                far_sum = as_column(partner_pack[a, n + 1 : n + 2], eye)
                near_top = m_ref[here, :]
                top = jnp.maximum(far_top, near_top)
                far_factor, factor = jnp.exp2(far_top - top), jnp.exp2(near_top - top)
                o = partner_pack[a, :n] * far_factor + o_ref[here, :] * factor
                packed(out_ref, a, o, top, far_sum * far_factor + l_ref[here, :] * factor)
            return carry

        lax.fori_loop(0, rows // step, finish, 0)

    for when, copy in sent:
        pl.when(when)(copy.wait_send)


def merge_kernel(far_ref, o_ref, m_ref, l_ref, out_ref, mixed_ref):
    heads, n, width = o_ref.shape
    row, col = grids(n)
    for g in range(heads):
        far_top = as_column(far_ref[g, n : n + 1], row == col)
        far_sum = as_column(far_ref[g, n + 1 : n + 2], row == col)
        near_top = m_ref[g]
        top = jnp.maximum(far_top, near_top)
        far_factor, near_factor = jnp.exp2(far_top - top), jnp.exp2(near_top - top)
        total = far_sum * far_factor + l_ref[g] * near_factor
        mixed = far_ref[g, :n] * far_factor + o_ref[g] * near_factor
        mixed_ref[g] = mixed / total
    turned(mixed_ref, out_ref)


def shape(*dims, dtype=F32):
    return jax.ShapeDtypeStruct(dims, dtype)


def call(kernel, out_shape, *operands, scratch=(), in_specs=None, **params):
    return pl.pallas_call(
        kernel,
        out_shape=out_shape,
        in_specs=in_specs or [pl.BlockSpec(memory_space=pltpu.VMEM)] * len(operands),
        out_specs=jax.tree.map(lambda _: pl.BlockSpec(memory_space=pltpu.VMEM), out_shape),
        scratch_shapes=list(scratch),
        compiler_params=pltpu.CompilerParams(vmem_limit_bytes=VMEM_LIMIT, **params),
    )(*operands)


def body(query, key, value, raw_directions, beta_raw_logits):
    n, heads, width = query.shape
    kv_heads = key.shape[1]
    blocks = lax.axis_size("key")
    sections = lax.axis_size("sec")
    rows = n * blocks
    scale = width ** (-0.5) * math.log2(math.e)
    vmem, dma = pltpu.VMEM, pltpu.SemaphoreType.DMA
    near, z, qw, section_query, section_kv, section_map = call(
        functools.partial(exchange_kernel, scale),
        [
            shape(blocks, 4, n, width),
            shape(kv_heads, n, n),
            shape(heads, n, n),
            shape(rows, width),
            shape(rows, 2 * width),
            shape(width, width),
        ],
        query, key, value, raw_directions, beta_raw_logits,
        scratch=[
            vmem((heads, n, width), BF16),
            vmem((kv_heads, n, width), BF16),
            vmem((kv_heads, n, width), BF16),
            vmem((kv_heads, 3, n, width), F32),
            vmem((heads, n, width), F32),
            dma((blocks, 4)),
            dma((blocks, 4)),
        ],
        collective_id=1,
        has_side_effects=True,
    )
    own = call(
        functools.partial(diagonal_kernel, scale),
        [shape(heads, n, width), shape(heads, n, 1), shape(heads, n, 1)],
        query, key, value, z, qw,
        scratch=[vmem((count, n, width), BF16) for count in (heads, kv_heads, kv_heads)],
    )
    back = call(
        section_kernel,
        shape(blocks, n + WIDE, width),
        near, section_query, section_kv, section_map,
        scratch=[
            vmem((6, rows, 2 * width), F32),
            vmem((sections, width, width), F32),
            vmem((4, rows, 4 * width), BF16),
            vmem((rows, width), F32),
            vmem((width, width), F32),
            vmem((rows, width), F32),
            vmem((3, rows, 4 * width), BF16),
            vmem((3, rows, width), BF16),
            vmem((2 * rows, width), F32),
            vmem((2 * rows, 1), F32),
            vmem((2 * rows, 1), F32),
            vmem((blocks, n + WIDE, width), F32),
            vmem((blocks, n + WIDE, width), F32),
            dma,
            dma((28,)),
            dma((sections, 4)),
            dma((sections - 1,)),
            dma((sections,)),
            dma((2,)),
            dma((4,)),
            dma((4,)),
        ],
        collective_id=0,
        has_side_effects=True,
    )
    far = lax.all_to_all(back, "key", split_axis=0, concat_axis=0, tiled=True)
    out = shape(n, heads, width, dtype=BF16)
    return call(merge_kernel, out, far, *own, scratch=[vmem((heads, n, width), F32)])


def solution(mesh):
    spec = P(("sec", "key"), None, None)
    return jax.shard_map(
        body,
        mesh=mesh,
        in_specs=(spec, spec, spec, spec, P(("sec", "key"), None)),
        out_specs=spec,
        check_vma=False,
    )
```

```python
import functools
import math

import jax
import jax.numpy as jnp
from jax import lax
from jax.experimental import pallas as pl
from jax.experimental.pallas import tpu as pltpu
from jax.sharding import PartitionSpec as P

F32 = jnp.float32
BF16 = jnp.bfloat16
NN = ((1,), (0,))
NT = ((1,), (1,))
TN = ((0,), (0,))
LOW = -1e30
VMEM_LIMIT = 56 * 1024 * 1024
WIDE = 8


def halves(x):
    high = x.astype(BF16)
    return high, (x - high.astype(F32)).astype(BF16)


def left(x, axis):
    high, low = halves(x)
    return jnp.concatenate([high, low, high, low], axis)


def right(x, axis):
    high, low = halves(x)
    return jnp.concatenate([high, high, low, low], axis)


def mm(a, b, dims):
    return lax.dot_general(a, b, (dims, ((), ())), preferred_element_type=F32)


def fine(a, b, dims):
    return mm(left(a, dims[0][0]), right(b, dims[1][0]), dims)


def grids(n):
    return lax.broadcasted_iota(jnp.int32, (n, n), 0), lax.broadcasted_iota(jnp.int32, (n, n), 1)


def as_row(column, eye):
    return jnp.sum(jnp.where(eye, column, 0.0), 0, keepdims=True)


def as_column(row, eye):
    return jnp.sum(jnp.where(eye, row, 0.0), 1, keepdims=True)


def turned(source, target):
    target[...] = jnp.swapaxes(source[...].astype(F32), 0, 1).astype(target.dtype)


def exchange_kernel(
    scale, q_in, k_in, v_in, w_in, b_ref,
    near_ref, z_ref, qw_ref, qs_ref, kvs_ref, map_ref,
    q_ref, k_ref, w_ref, shared, starts, send_sems, recv_sems,
):
    blocks = near_ref.shape[0]
    section, me = lax.axis_index("sec"), lax.axis_index("key")
    mesh_ids = pl.DeviceIdType.MESH
    barrier = pltpu.get_barrier_semaphore()

    def greet(d, carry):
        device = (section, (me + d) % blocks)
        pl.semaphore_signal(barrier, inc=1, device_id=device, device_id_type=mesh_ids)
        return carry

    lax.fori_loop(1, blocks, greet, 0)
    pl.semaphore_wait(barrier, blocks - 1)
    heads, n, width = k_ref.shape
    group = q_ref.shape[0] // heads
    row, col = grids(n)

    def outgoing(to, piece):
        return pltpu.make_async_remote_copy(
            src_ref=starts.at[to] if piece == 0 else shared.at[to // group, piece - 1],
            dst_ref=near_ref.at[me, piece],
            send_sem=send_sems.at[to, piece],
            recv_sem=recv_sems.at[me, piece],
            device_id=(section, to),
            device_id_type=mesh_ids,
        )

    def send(piece):
        def one(d, carry):
            outgoing((me + d) % blocks, piece).start()
            return carry

        lax.fori_loop(1, blocks, one, 0)

    def arrive(piece):
        def one(d, carry):
            source = (me + d) % blocks
            outgoing(source, piece).wait_send()
            pltpu.make_async_remote_copy(
                src_ref=starts.at[source],
                dst_ref=near_ref.at[source, piece],
                send_sem=send_sems.at[source, piece],
                recv_sem=recv_sems.at[source, piece],
                device_id=(section, source),
                device_id_type=mesh_ids,
            ).wait_recv()
            return carry

        lax.fori_loop(1, blocks, one, 0)

    shared[:, 1] = jnp.swapaxes(v_in[...].astype(F32), 0, 1)
    near_ref[me, 2] = shared[me // group, 1]
    send(2)
    turned(q_in, q_ref)
    turned(k_in, k_ref)
    turned(w_in, w_ref)
    units, betas, lows, inverses = [], [], [], []
    for h in range(heads):
        w = w_ref[h].astype(F32)
        unit = w / jnp.sqrt(jnp.sum(w * w, -1, keepdims=True) + 1e-6)
        beta = 2.0 / (1.0 + jnp.exp(-b_ref[:, h : h + 1]))
        low = jnp.where(row > col, beta * fine(unit, unit, NT), 0.0)
        first = ((row ^ col) == 1) & (row > col)
        units.append(unit)
        betas.append(beta)
        lows.append(low)
        inverses.append(jnp.where(row == col, 1.0, jnp.where(first, -low, 0.0)))
    size = 2
    while size < n:
        pick = ((row ^ col) < 2 * size) & ((row & size) != 0) & ((col & size) == 0)
        inner = [fine(jnp.where(pick, lows[h], 0.0), inverses[h], NN) for h in range(heads)]
        inverses = [inverses[h] - fine(inverses[h], inner[h], NN) for h in range(heads)]
        size *= 2
    ys, sides = [], []
    for h in range(heads):
        unit, beta, inverse = units[h], betas[h], inverses[h]
        key = k_ref[h]
        high, low = halves(unit)
        both = jnp.concatenate([high, low], 1)
        cross = jnp.where(row > col, mm(both, jnp.concatenate([key, key], 1), NT), 0.0)
        solved = fine(inverse, jnp.concatenate([beta * unit, beta * cross], 1), NN)
        y, z = solved[:, :width], solved[:, width:]
        z_ref[h] = z
        ys.append(right(y, 0))
        sides.append(both)
        shared[h, 2] = jnp.where(row == col, 1.0, 0.0) - fine(unit, y, TN)
        shared[h, 0] = key.astype(F32) - fine(z, unit, TN)
    near_ref[me, 3] = shared[me // group, 2]
    near_ref[me, 1] = shared[me // group, 0]
    send(3)
    send(1)
    for h in range(heads):
        for g in range(h * group, h * group + group):
            query = q_ref[g]
            qw = jnp.where(row >= col, mm(jnp.concatenate([query, query], 1), sides[h], NT), 0.0)
            qw_ref[g] = qw
            starts[g] = (query.astype(F32) - mm(left(qw, 1), ys[h], NN)) * scale
    near_ref[me, 0] = starts[me]
    send(0)

    arrive(3)
    pairs = [fine(near_ref[2 * g + 1, 3], near_ref[2 * g, 3], NN) for g in range(blocks // 2)]
    before, after = [None], [None] * blocks
    reach = None
    for g in range(blocks // 2):
        even, b = near_ref[2 * g, 3], blocks // 2 - 1 - g
        before.append(even if g == 0 else fine(even, before[2 * g], NN))
        before.append(pairs[g] if g == 0 else fine(pairs[g], before[2 * g], NN))
        after[2 * b + 1] = reach
        odd = near_ref[2 * b + 1, 3]
        after[2 * b] = odd if g == 0 else fine(reach, odd, NN)
        reach = pairs[b] if g == 0 else fine(reach, pairs[b], NN)
    map_ref[...] = before[blocks]
    arrive(1)
    for b in range(blocks):
        key = near_ref[b, 1]
        kvs_ref[b * n : b * n + n, :width] = key if after[b] is None else fine(key, after[b], NT)
    arrive(2)
    for b in range(blocks):
        kvs_ref[b * n : b * n + n, width:] = near_ref[b, 2]
    arrive(0)
    for a in range(blocks):
        query = near_ref[a, 0]
        qs_ref[a * n : a * n + n] = query if a == 0 else fine(query, before[a], NN)


def diagonal_kernel(scale, q_in, k_in, v_in, z_ref, qw_ref, o_ref, m_ref, l_ref, q_ref, k_ref, v_ref):
    heads, n, width = k_ref.shape
    turned(q_in, q_ref)
    turned(k_in, k_ref)
    turned(v_in, v_ref)
    group = q_ref.shape[0] // heads
    row, col = grids(n)
    for h in range(heads):
        z_right = right(z_ref[h], 0)
        for g in range(h * group, h * group + group):
            score = mm(q_ref[g], k_ref[h], NT) - mm(left(qw_ref[g], 1), z_right, NN)
            score = jnp.where(row >= col, score * scale, LOW)
            top = jnp.max(score, -1, keepdims=True)
            weight = jnp.exp2(score - top)
            m_ref[g] = top
            l_ref[g] = jnp.sum(weight, -1, keepdims=True)
            o_ref[g] = mm(weight.astype(BF16), v_ref[h], NN)


def near_attention(x_ref, key_ref, cat_ref, value_ref, store):
    blocks, _, n, width = x_ref.shape
    pair = 2 * n
    for g in range(blocks // 2):
        first, second, past = 2 * g, 2 * g + 1, g * pair
        if g > 0:
            old = past - pair
            if g > 1:
                both = fine(x_ref[first - 1, 3], x_ref[first - 2, 3], NN)
                key_ref[:old] = mm(cat_ref[:old], left(both, 1), NT)
            key_ref[old : old + n] = fine(x_ref[first - 2, 1], x_ref[first - 1, 3], NT)
            key_ref[old + n : past] = x_ref[first - 1, 1]
            value_ref[old : old + n] = x_ref[first - 2, 2].astype(BF16)
            value_ref[old + n : past] = x_ref[first - 1, 2].astype(BF16)
            cat_ref[:past] = right(key_ref[:past], 1)
        later = x_ref[second, 0]
        inner = fine(later, x_ref[first, 1], NT)
        inner_value = x_ref[first, 2].astype(BF16)
        inner_top = jnp.max(inner, -1, keepdims=True)
        if g == 0:
            weight = jnp.exp2(inner - inner_top)
            store(0, jnp.zeros((n, width), F32), jnp.full((n, 1), LOW, F32), jnp.zeros((n, 1), F32))
            o = mm(weight.astype(BF16), inner_value, NN)
            store(1, o, inner_top, jnp.sum(weight, -1, keepdims=True))
            continue
        query = jnp.concatenate([x_ref[first, 0], fine(later, x_ref[first, 3], NN)], 0)
        score = mm(left(query, 1), cat_ref[:past], NT)
        top = jnp.max(score, -1, keepdims=True)
        top = jnp.concatenate([top[:n], jnp.maximum(top[n:], inner_top)], 0)
        weight = jnp.exp2(score - top)
        inner_weight = jnp.exp2(inner - top[n:])
        total = jnp.sum(weight, -1, keepdims=True)
        o = mm(weight.astype(BF16), value_ref[:past], NN)
        store(first, o[:n], top[:n], total[:n])
        inner_o = mm(inner_weight.astype(BF16), inner_value, NN)
        store(second, o[n:] + inner_o, top[n:], total[n:] + jnp.sum(inner_weight, -1, keepdims=True))


def section_kernel(
    x_ref, q_in, kv_ref, map_ref, out_ref,
    all_kv, maps, frames, partner_q, product, key_ref, cats, values,
    o_ref, m_ref, l_ref, pack, partner_pack,
    local_sem, kv_send, kv_recv, map_send, map_recv, q_sems, pack_send, pack_recv,
):
    blocks, _, n, width = x_ref.shape
    rows = blocks * n
    quarter_rows, step = rows // 4, 512
    sections = maps.shape[0]
    chips = sections // 2
    s, k = lax.axis_index("sec"), lax.axis_index("key")
    x, c = s // 2, s % 2
    z = k % 4
    sibling, partner = s + 1 - 2 * c, sections - 1 - s
    helper = s < sections // 2
    ahead_chip, behind_chip, across_chip = (x + 1) % chips, (x + chips - 1) % chips, (x + 2) % chips
    ahead, behind, across = (chip * 2 + c for chip in (ahead_chip, behind_chip, across_chip))
    z_next, z_last = k - z + (z + 1) % 4, k - z + (z + 3) % 4
    mine, other = z % 2 * 2, 2 - z % 2 * 2
    mesh_ids = pl.DeviceIdType.MESH

    def need(t, chip):
        return (
            ((chip == 0) & (t == 2))
            | ((chip == 1) & (t < 2))
            | ((chip == 2) & ((t < 2) | (t == 3)))
            | ((chip == 3) & (t >= 3) & (t <= 5))
        )

    def place(t, quarter):
        return all_kv.at[t % 6, pl.ds(pl.multiple_of(quarter * quarter_rows, quarter_rows), quarter_rows)]

    sent = []

    def put(when, t, quarter, device, source=None):
        copy = pltpu.make_async_remote_copy(
            src_ref=place(t, quarter) if source is None else source,
            dst_ref=place(t, quarter),
            send_sem=kv_send.at[len(sent)],
            recv_sem=kv_recv.at[t, quarter],
            device_id=device,
            device_id_type=mesh_ids,
        )
        pl.when(when)(copy.start)
        sent.append((when, copy))

    def got(when, t, quarter):
        copy = pltpu.make_async_remote_copy(
            src_ref=place(t, quarter),
            dst_ref=place(t, quarter),
            send_sem=kv_send.at[0],
            recv_sem=kv_recv.at[t, quarter],
            device_id=(sibling, k),
            device_id_type=mesh_ids,
        )
        pl.when(when)(copy.wait_recv)

    others = [(s + d) % sections for d in range(1, sections)]
    barrier = pltpu.get_barrier_semaphore()
    greeted = [(t, k) for t in others] + [(s, z_next), (s, z_last)]
    for device in greeted:
        pl.semaphore_signal(barrier, inc=1, device_id=device, device_id_type=mesh_ids)
    pl.semaphore_wait(barrier, len(greeted))

    map_copies = [
        pltpu.make_async_remote_copy(
            src_ref=map_ref,
            dst_ref=maps.at[s],
            send_sem=map_send.at[d],
            recv_sem=map_recv.at[s],
            device_id=(t, k),
            device_id_type=mesh_ids,
        )
        for d, t in enumerate(others)
    ]
    for copy in map_copies:
        copy.start()
    own_copy = pltpu.make_async_copy(kv_ref, all_kv.at[s % 6], local_sem)
    pl.when(helper)(own_copy.start)
    for index in range(2):
        source = kv_ref.at[pl.ds(pl.multiple_of((mine + index) * quarter_rows, quarter_rows), quarter_rows)]
        onward = need(s, across_chip)
        put(need(s, ahead_chip) | (onward & (index == 0)), s, mine + index, (ahead, k), source)
        put(need(s, behind_chip) | (onward & (index == 1)), s, mine + index, (behind, k), source)
    query_copy = pltpu.make_async_remote_copy(
        src_ref=q_in,
        dst_ref=partner_q,
        send_sem=q_sems.at[0],
        recv_sem=q_sems.at[1],
        device_id=(partner, k),
        device_id_type=mesh_ids,
    )
    pl.when(jnp.logical_not(helper))(query_copy.start)
    for quarter in range(4):
        source = kv_ref.at[quarter * quarter_rows : (quarter + 1) * quarter_rows]
        put(s != sections - 1, s, quarter, (sibling, k), source)

    def pass_mine(t, index, onward, onward_when):
        here = need(t, x)
        got(here | onward_when, t, mine + index)
        if onward is not None:
            put(onward_when, t, mine + index, (onward, k))
        put(here, t, mine + index, (s, z_last if index else z_next))
        put(here, t, mine + index, (sibling, k))

    def pass_other(t, index, when=True):
        got(need(t, x) & when, t, other + index)
        put(need(t, x) & when, t, other + index, (sibling, k))

    def store(a, o, m, l):
        at = slice(a * n, a * n + n)
        o_ref[at], m_ref[at], l_ref[at] = o, m, l

    near_attention(x_ref, key_ref, cats.at[0], values.at[0], store)
    pass_mine(behind, 0, ahead, need(behind, ahead_chip))
    pass_mine(ahead, 0, None, False)
    o_ref[rows:] = jnp.zeros((rows, width), F32)
    m_ref[rows:] = jnp.full((rows, 1), LOW, F32)
    l_ref[rows:] = jnp.zeros((rows, 1), F32)

    maps[s] = map_ref[...]
    for d, t in enumerate(others):
        map_copies[d].wait_send()
        pltpu.make_async_remote_copy(
            src_ref=map_ref,
            dst_ref=maps.at[t],
            send_sem=map_send.at[d],
            recv_sem=map_recv.at[t],
            device_id=(t, k),
            device_id_type=mesh_ids,
        ).wait_recv()

    def helped(owner, t):
        return ((owner >= 6) & (t <= 2)) | (((owner == 4) | (owner == 5)) & (t == 2))

    def own_slot(t):
        return t - jnp.where(s >= 6, 3, jnp.where((s >= 4) & (t > 2), 1, 0))

    def helper_slot(t):
        return jnp.where(s < 2, s + t, s)

    def build(q_ref, count, wanted, slot):
        def turn(index, carry):
            t = count - 1 - index

            @pl.when(wanted(t) & (index == 0))
            def _():
                frames[slot(t)] = left(q_ref[...], 1)

            @pl.when(wanted(t) & (index > 0))
            def _():
                frames[slot(t)] = left(fine(q_ref[...], product[...], NN), 1)

            @pl.when((index == 0) & (t > 0))
            def _():
                product[...] = maps[t]

            @pl.when((index > 0) & (t > 0))
            def _():
                product[...] = fine(product[...], maps[t], NN)

            return carry

        lax.fori_loop(0, count, turn, 0)

    build(q_in, s, lambda t: jnp.logical_not(helped(s, t)), own_slot)
    pass_mine(ahead, 1, behind, need(ahead, behind_chip))
    pass_mine(behind, 1, None, False)

    @pl.when(helper)
    def _():
        query_copy.wait_recv()
        build(partner_q, partner, lambda t: helped(partner, t), helper_slot)

    def attend_rows(query, here, slot):
        score = mm(query, cats[slot], NT)
        old = m_ref[here, :]
        top = jnp.maximum(old, jnp.max(score, -1, keepdims=True))
        weight = jnp.exp2(score - top)
        factor = jnp.exp2(old - top)
        m_ref[here, :] = top
        l_ref[here, :] = l_ref[here, :] * factor + jnp.sum(weight, -1, keepdims=True)
        o_ref[here, :] = o_ref[here, :] * factor + mm(weight.astype(BF16), values[slot], NN)

    def convert(t, slot):
        cats[slot] = right(all_kv[t % 6, :, :width], 1)
        values[slot] = all_kv[t % 6, :, width:].astype(BF16)

    def tile(t):
        @pl.when((t < s) & jnp.logical_not(helped(s, t)))
        def _():
            convert(t, 0)

            def part(at, carry):
                here = pl.ds(pl.multiple_of(at * step, step), step)
                attend_rows(frames[own_slot(t), here, :], here, 0)
                return carry

            lax.fori_loop(0, rows // step, part, 0)

    for quarter in range(4):
        got(sibling != sections - 1, sibling, quarter)
    tile(sibling)
    for index in range(2):
        pass_other(behind, index)
        pass_other(ahead, index)
    pass_mine(across, 0, None, False)
    pass_mine(across, 1, None, False)

    row, col = grids(n)
    eye = row == col
    part_blocks = step // n

    def packed(target, a, o, m, l):
        target[a, :n] = o
        target[a, n : n + 1] = as_row(m, eye)
        target[a, n + 1 : n + 2] = as_row(l, eye)
        target[a, n + 2 :] = jnp.zeros((WIDE - 2, width), F32)

    def pack_copy(at):
        piece = pl.ds(at * part_blocks, part_blocks)
        return pltpu.make_async_remote_copy(
            src_ref=pack.at[piece],
            dst_ref=partner_pack.at[piece],
            send_sem=pack_send.at[at],
            recv_sem=pack_recv.at[at],
            device_id=(partner, k),
            device_id_type=mesh_ids,
        )

    @pl.when(helper)
    def _():
        own_copy.wait()
        first_slot = s < 2
        for quarter in range(4):
            got(s == 1, 2, quarter)
        count = jnp.where(first_slot, 3, 1)

        def prepare(index, carry):
            convert(jnp.where(first_slot, index, 2), index)
            return carry

        lax.fori_loop(0, count, prepare, 0)

        def rows_part(at, carry):
            here = pl.ds(pl.multiple_of(rows + at * step, step), step)

            def one(index, carry):
                frame = helper_slot(jnp.where(first_slot, index, 2))
                attend_rows(frames[frame, pl.ds(pl.multiple_of(at * step, step), step), :], here, index)
                return carry

            lax.fori_loop(0, count, one, 0)
            for block in range(part_blocks):
                these = pl.ds(pl.multiple_of(rows + at * step + block * n, n), n)
                packed(pack, at * part_blocks + block, o_ref[these, :], m_ref[these, :], l_ref[these, :])
            pack_copy(at).start()
            return carry

        lax.fori_loop(0, rows // step, rows_part, 0)

    beside_behind, beside_across = behind + 1 - 2 * c, across + 1 - 2 * c
    tile(behind)
    for index in range(2):
        pass_other(across, index, x == chips - 1)
    for quarter in range(4):
        got(need(beside_behind, x), beside_behind, quarter)
    tile(beside_behind)
    for index in range(2):
        pass_other(across, index, x != chips - 1)
    tile(across)
    for quarter in range(4):
        got(need(beside_across, x), beside_across, quarter)
    tile(beside_across)

    @pl.when(helper)
    def _():
        def finish(a, carry):
            here = pl.ds(pl.multiple_of(a * n, n), n)
            packed(out_ref, a, o_ref[here, :], m_ref[here, :], l_ref[here, :])
            return carry

        lax.fori_loop(0, blocks, finish, 0)
        for at in range(rows // step):
            pack_copy(at).wait_send()

    @pl.when(jnp.logical_not(helper))
    def _():
        query_copy.wait_send()

        def finish(at, carry):
            pack_copy(at).wait_recv()
            for block in range(part_blocks):
                a = at * part_blocks + block
                here = pl.ds(pl.multiple_of(a * n, n), n)
                far_top = as_column(partner_pack[a, n : n + 1], eye)
                far_sum = as_column(partner_pack[a, n + 1 : n + 2], eye)
                near_top = m_ref[here, :]
                top = jnp.maximum(far_top, near_top)
                far_factor, factor = jnp.exp2(far_top - top), jnp.exp2(near_top - top)
                o = partner_pack[a, :n] * far_factor + o_ref[here, :] * factor
                packed(out_ref, a, o, top, far_sum * far_factor + l_ref[here, :] * factor)
            return carry

        lax.fori_loop(0, rows // step, finish, 0)

    for when, copy in sent:
        pl.when(when)(copy.wait_send)


def merge_kernel(far_ref, o_ref, m_ref, l_ref, out_ref, mixed_ref):
    heads, n, width = o_ref.shape
    row, col = grids(n)
    for g in range(heads):
        far_top = as_column(far_ref[g, n : n + 1], row == col)
        far_sum = as_column(far_ref[g, n + 1 : n + 2], row == col)
        near_top = m_ref[g]
        top = jnp.maximum(far_top, near_top)
        far_factor, near_factor = jnp.exp2(far_top - top), jnp.exp2(near_top - top)
        total = far_sum * far_factor + l_ref[g] * near_factor
        mixed = far_ref[g, :n] * far_factor + o_ref[g] * near_factor
        mixed_ref[g] = mixed / total
    turned(mixed_ref, out_ref)


def shape(*dims, dtype=F32):
    return jax.ShapeDtypeStruct(dims, dtype)


def call(kernel, out_shape, *operands, scratch=(), in_specs=None, **params):
    return pl.pallas_call(
        kernel,
        out_shape=out_shape,
        in_specs=in_specs or [pl.BlockSpec(memory_space=pltpu.VMEM)] * len(operands),
        out_specs=jax.tree.map(lambda _: pl.BlockSpec(memory_space=pltpu.VMEM), out_shape),
        scratch_shapes=list(scratch),
        compiler_params=pltpu.CompilerParams(vmem_limit_bytes=VMEM_LIMIT, **params),
    )(*operands)


def body(query, key, value, raw_directions, beta_raw_logits):
    n, heads, width = query.shape
    kv_heads = key.shape[1]
    blocks = lax.axis_size("key")
    sections = lax.axis_size("sec")
    rows = n * blocks
    scale = width ** (-0.5) * math.log2(math.e)
    vmem, dma = pltpu.VMEM, pltpu.SemaphoreType.DMA
    near, z, qw, section_query, section_kv, section_map = call(
        functools.partial(exchange_kernel, scale),
        [
            shape(blocks, 4, n, width),
            shape(kv_heads, n, n),
            shape(heads, n, n),
            shape(rows, width),
            shape(rows, 2 * width),
            shape(width, width),
        ],
        query, key, value, raw_directions, beta_raw_logits,
        scratch=[
            vmem((heads, n, width), BF16),
            vmem((kv_heads, n, width), BF16),
            vmem((kv_heads, n, width), BF16),
            vmem((kv_heads, 3, n, width), F32),
            vmem((heads, n, width), F32),
            dma((blocks, 4)),
            dma((blocks, 4)),
        ],
        collective_id=1,
        has_side_effects=True,
    )
    own = call(
        functools.partial(diagonal_kernel, scale),
        [shape(heads, n, width), shape(heads, n, 1), shape(heads, n, 1)],
        query, key, value, z, qw,
        scratch=[vmem((count, n, width), BF16) for count in (heads, kv_heads, kv_heads)],
    )
    back = call(
        section_kernel,
        shape(blocks, n + WIDE, width),
        near, section_query, section_kv, section_map,
        scratch=[
            vmem((6, rows, 2 * width), F32),
            vmem((sections, width, width), F32),
            vmem((4, rows, 4 * width), BF16),
            vmem((rows, width), F32),
            vmem((width, width), F32),
            vmem((rows, width), F32),
            vmem((3, rows, 4 * width), BF16),
            vmem((3, rows, width), BF16),
            vmem((2 * rows, width), F32),
            vmem((2 * rows, 1), F32),
            vmem((2 * rows, 1), F32),
            vmem((blocks, n + WIDE, width), F32),
            vmem((blocks, n + WIDE, width), F32),
            dma,
            dma((30,)),
            dma((sections, 4)),
            dma((sections - 1,)),
            dma((sections,)),
            dma((2,)),
            dma((4,)),
            dma((4,)),
        ],
        collective_id=0,
        has_side_effects=True,
    )
    far = lax.all_to_all(back, "key", split_axis=0, concat_axis=0, tiled=True)
    out = shape(n, heads, width, dtype=BF16)
    return call(merge_kernel, out, far, *own, scratch=[vmem((heads, n, width), F32)])


def solution(mesh):
    spec = P(("sec", "key"), None, None)
    return jax.shard_map(
        body,
        mesh=mesh,
        in_specs=(spec, spec, spec, spec, P(("sec", "key"), None)),
        out_specs=spec,
        check_vma=False,
    )
```
